256 devices in a mesh: dp: 16 (over z, core), seq: 16 (over y, x).
Axes of the slice: x: 4, y: 4, z: 8, core: 2. Of those that a mesh axis runs over, the one named last changes fastest.
Arguments:
- tokens: bfloat16 [32768, 2560], P(('dp', 'seq')), may hold values from -6 to 6
- modulation: float32 [4, 128, 2560], P(None, 'dp'), may hold values from -3 to 3
- img_size: int32 [16, 8], replicated, may hold values from 0 to 2048, as said below
- text_count: int32 [16, 8], replicated, may hold values from 0 to 128, as said below
- move_list: int32 [16, 4, 2], replicated, may hold values from 0 to 15, as said below
- w_qkv: bfloat16 [2560, 6144], P('dp', 'seq'), may hold values from -0.125 to 0.125
- qk_gain: float32 [2, 2048], P(None, 'seq'), may hold values from 0.1 to 1.9
- cotangent: bfloat16 [32768, 2048], P(('dp', 'seq')), may hold values from -6 to 6
Outputs:
- attended: bfloat16 [32768, 2048], P('dp', 'seq')
- grad_w: float32 [2560, 6144], P('dp', 'seq')
The draws below stay inside these ranges and needn't reach their ends.
Inputs may be any that keep to these rules, and one draw needn't show every extreme that they name: `img_size`: in every group the used slots come first and tile its 2048 rows in order; every used size is 128 times a power of two, at least 256, and each image starts at a multiple of its size; unused slots are 0. `text_count`: at least 1 for a used slot, 0 for an unused one. `move_list`: in each column the 4 entries name 4 distinct groups and form one cycle: each entry's destination is the next entry's source and the last's is the first's.
All inputs are finite; a program needn't handle non-finite values.
Results may differ from the reference program's by a relative error of at most 0.014.
Values may be sent and summed in bfloat16 or wider, within the bound.
A program may use at most 128 MiB of HBM per device.

```python
import jax
import jax.numpy as jnp
from jax import lax

D = 2560
DH = 128
ROWS_DEV = 128
MOVES = 4
HEADS = 16
IMG_GRP = 8
TOKENS = 32768
N_DP = 16
N_SEQ = 16


def group_layout(key):
    split_key, whole_key, text_key, longest_key = jax.random.split(key, 4)
    group_ids = jnp.arange(N_DP, dtype=jnp.int32)
    column_ids = jnp.arange(N_SEQ, dtype=jnp.int32)
    run_length = jnp.full((N_DP, N_SEQ), N_SEQ, jnp.int32)
    level_span = N_SEQ
    level_number = 0
    while level_span > 2:
        child_span = level_span // 2
        split_bits = jax.random.randint(jax.random.fold_in(split_key, level_number), (N_DP, N_SEQ // level_span), 0, 2)
        node_bits = jnp.repeat(split_bits, level_span, axis=1)
        run_length = jnp.where((run_length == level_span) & (node_bits == 1), child_span, run_length)
        level_span = child_span
        level_number = level_number + 1
    whole_group = jax.random.randint(whole_key, (), 0, N_DP)
    run_length = jnp.where(group_ids[:, None] == whole_group, N_SEQ, run_length)
    is_start = (column_ids[None, :] % run_length == 0).astype(jnp.int32)
    image_slot = jnp.cumsum(is_start, axis=1) - 1
    slot_ids = jnp.arange(IMG_GRP, dtype=jnp.int32)
    owners = (image_slot[:, :, None] == slot_ids[None, None, :]).astype(jnp.int32) * is_start[:, :, None]
    image_sizes = jnp.sum(owners * run_length[:, :, None], axis=1) * ROWS_DEV
    text_counts = jax.random.randint(text_key, (N_DP, IMG_GRP), 1, ROWS_DEV + 1)
    text_counts = jnp.where(image_sizes > 0, text_counts, 0)
    longest_group = jax.random.randint(longest_key, (), 0, N_DP)
    text_counts = jnp.where((group_ids[:, None] == longest_group) & (slot_ids[None, :] == 0), ROWS_DEV, text_counts)
    return (image_sizes.astype(jnp.int32), text_counts.astype(jnp.int32))


def draw_img_size(key, part):
    return group_layout(key)[0]


def draw_text_count(key, part):
    return group_layout(key)[1]


def draw_move_list(key, part):
    key = jax.random.fold_in(key, 11)
    column_keys = jax.random.split(key, N_SEQ)
    orders = jax.vmap(lambda column_key: jax.random.permutation(column_key, N_DP))(column_keys)
    chosen = orders[:, :MOVES].astype(jnp.int32)
    return jnp.stack([chosen, jnp.roll(chosen, -1, axis=1)], axis=2).astype(jnp.int32)


def level_of(stream_key, extent, cuts, low, largest):
    gain, own = 1.0, jax.random.fold_in(stream_key, 6)
    for position, parts in cuts:
        steps = jnp.exp(jax.random.uniform(jax.random.fold_in(own, position), (parts,), jnp.float32, low / len(cuts), largest / len(cuts)))
        gain = gain * jnp.repeat(steps, extent[position] // parts).reshape([-1 if axis == position else 1 for axis in range(len(extent))])
    return gain


def gaussian(own_key, extent, scale, reach, cuts=(), kind=jnp.bfloat16):
    drawn = scale * jax.random.normal(own_key, extent, jnp.float32)
    if cuts:
        drawn = drawn * level_of(own_key, extent, cuts, -0.22, 0.18)
    return jnp.clip(drawn, -reach, reach).astype(kind)


def setup_inputs(seed: int = 0) -> dict:
    streams_of = jax.random.split(jax.random.key(seed), 9)
    tokens = gaussian(streams_of[0], (TOKENS, D), 1.0, 6.0, ((0, 256),))
    modulation = gaussian(streams_of[1], (4, N_DP * IMG_GRP, D), 0.5, 3.0, ((1, 16),), jnp.float32)
    img_size = draw_img_size(jax.random.fold_in(streams_of[8], 71), 0)
    text_count = draw_text_count(jax.random.fold_in(streams_of[8], 71), 0)
    move_list = draw_move_list(jax.random.fold_in(streams_of[8], 71), 0)
    w_qkv = gaussian(streams_of[5], (D, HEADS * 3 * DH), D ** -0.5, 0.125, ((0, 16), (1, 16)))
    qk_gain = jnp.clip(1.0 + 0.18 * jax.random.normal(streams_of[6], (2, HEADS * DH), jnp.float32), 0.1, 1.9)
    cotangent = gaussian(streams_of[7], (TOKENS, HEADS * DH), 1.0, 6.0, ((0, 256),))
    return dict(tokens=tokens, modulation=modulation, img_size=img_size, text_count=text_count, move_list=move_list, w_qkv=w_qkv, qk_gain=qk_gain, cotangent=cotangent)


EPSILON = 1e-06

def home_layout(img_size, text_count, group_rows):
    positions = jnp.arange(group_rows, dtype=jnp.int32)
    image_ends = jnp.cumsum(img_size, axis=1).astype(jnp.int32)
    image_index = lax.optimization_barrier(jnp.sum((positions[None, :, None] >= image_ends[:, None, :]).astype(jnp.int32), axis=2)).astype(jnp.int32)
    slot_ids = jnp.arange(img_size.shape[1], dtype=jnp.int32)
    owners = (image_index[:, :, None] == slot_ids[None, None, :]).astype(jnp.int32)
    starts = lax.optimization_barrier(jnp.sum(owners * (image_ends - img_size)[:, None, :], axis=2))
    limits = lax.optimization_barrier(jnp.sum(owners * text_count[:, None, :], axis=2))
    is_text = positions[None, :] - starts < limits
    return (image_index, is_text)

def sources(move_list, group_count):
    group_ids = jnp.arange(group_count, dtype=jnp.int32)
    move_hits = (group_ids[:, None, None] == move_list[None, :, :, 1]).astype(jnp.int32)
    is_moved = lax.optimization_barrier(jnp.sum(move_hits, axis=2)) > 0
    anchor = lax.optimization_barrier(jnp.sum(move_hits * move_list[None, :, :, 0], axis=2)).astype(jnp.int32)
    return jnp.where(is_moved, anchor, group_ids[:, None]).astype(jnp.int32)

def rms_scale(values, gain_row):
    inverse = lax.rsqrt(lax.optimization_barrier(jnp.mean(values * values, axis=-1, keepdims=True)) + EPSILON)
    return (values * inverse * gain_row, inverse)

def rms_back(values, inverse, gain_row, upstream):
    inner_mean = lax.optimization_barrier(jnp.mean(upstream * gain_row * values, axis=-1, keepdims=True))
    return inverse * gain_row * upstream - values * (inverse * inverse * inverse) * inner_mean

def head_pass(gathered, segment, weight, gain_pair, upstream):
    score_scale = 1.0 / DH ** 0.5
    projected = jnp.dot(gathered, weight, preferred_element_type=jnp.float32)
    query_raw = projected[:, :DH]
    key_raw = projected[:, DH:2 * DH]
    value_raw = projected[:, 2 * DH:]
    query_norm, query_inverse = rms_scale(query_raw, gain_pair[0])
    key_norm, key_inverse = rms_scale(key_raw, gain_pair[1])
    query_bf = query_norm.astype(jnp.bfloat16)
    key_bf = key_norm.astype(jnp.bfloat16)
    value_bf = value_raw.astype(jnp.bfloat16)
    scores = jnp.dot(query_bf, key_bf.T, preferred_element_type=jnp.float32) * score_scale
    same_image = segment[:, None] == segment[None, :]
    exponent = jnp.where(same_image, jnp.exp(scores), 0.0)
    probabilities = (exponent / lax.optimization_barrier(jnp.sum(exponent, axis=1, keepdims=True))).astype(jnp.bfloat16)
    attended = jnp.dot(probabilities, value_bf, preferred_element_type=jnp.float32).astype(jnp.bfloat16)
    row_delta = lax.optimization_barrier(jnp.sum(upstream.astype(jnp.float32) * attended.astype(jnp.float32), axis=1, keepdims=True))
    value_grad = jnp.dot(probabilities.T, upstream, preferred_element_type=jnp.float32)
    value_prob_grad = jnp.dot(upstream, value_bf.T, preferred_element_type=jnp.float32)
    score_grad = (probabilities.astype(jnp.float32) * (value_prob_grad - row_delta) * score_scale).astype(jnp.bfloat16)
    query_norm_grad = jnp.dot(score_grad, key_bf, preferred_element_type=jnp.float32)
    key_norm_grad = jnp.dot(score_grad.T, query_bf, preferred_element_type=jnp.float32)
    query_grad = rms_back(query_raw, query_inverse, gain_pair[0], query_norm_grad)
    key_grad = rms_back(key_raw, key_inverse, gain_pair[1], key_norm_grad)
    head_grads = jnp.concatenate([query_grad, key_grad, value_grad], axis=1).astype(jnp.bfloat16)
    weight_grad = lax.dot_general(gathered, head_grads, (((0,), (0,)), ((), ())), preferred_element_type=jnp.float32)
    return (attended, weight_grad)

def reference(tokens, modulation, img_size, text_count, move_list, w_qkv, qk_gain, cotangent):
    group_rows = N_SEQ * ROWS_DEV
    image_index, is_text = home_layout(img_size, text_count, group_rows)
    tokens_home = tokens.reshape(N_DP, group_rows, D)
    mod_groups = modulation.reshape(4, N_DP, IMG_GRP, D).transpose(1, 0, 2, 3)

    def modulate(group_in):
        token_block, group_mods, index_row, text_row = group_in
        token_rows = token_block.astype(jnp.float32)
        centre = lax.optimization_barrier(jnp.mean(token_rows, axis=1, keepdims=True))
        offsets = token_rows - centre
        variance = lax.optimization_barrier(jnp.mean(offsets * offsets, axis=1, keepdims=True))
        normed = offsets * lax.rsqrt(variance + EPSILON)
        picked = group_mods[:, index_row, :]
        shift_rows = jnp.where(text_row[:, None], picked[2], picked[0])
        scale_rows = jnp.where(text_row[:, None], picked[3], picked[1])
        return (normed * (1.0 + scale_rows) + shift_rows).astype(jnp.bfloat16)
    modulated = lax.map(modulate, (tokens_home, mod_groups, image_index, is_text))
    anchor = sources(move_list, N_DP)
    column_grid = jnp.broadcast_to(jnp.arange(N_SEQ, dtype=jnp.int32)[None, :], (N_DP, N_SEQ))
    moved = modulated.reshape(N_DP, N_SEQ, ROWS_DEV, D)[anchor, column_grid].reshape(N_DP, group_rows, D)
    moved_index = image_index.reshape(N_DP, N_SEQ, ROWS_DEV)[anchor, column_grid]
    segment = (anchor[:, :, None] * IMG_GRP + moved_index).reshape(N_DP, group_rows).astype(jnp.int32)
    weight_heads = w_qkv.reshape(D, HEADS, 3 * DH).transpose(1, 0, 2)
    gain_heads = qk_gain.reshape(2, HEADS, DH).transpose(1, 0, 2)
    upstream_all = cotangent.reshape(N_DP, group_rows, HEADS, DH).transpose(0, 2, 1, 3)

    def group_step(running, group_in):
        gathered, group_segment, group_upstream = group_in

        def one_head(head_in):
            weight, gain_pair, upstream = head_in
            return head_pass(gathered, group_segment, weight, gain_pair, upstream)
        attended_heads, grad_heads = lax.map(one_head, (weight_heads, gain_heads, group_upstream))
        return (running + grad_heads, attended_heads)
    initial = jnp.zeros((HEADS, D, 3 * DH), jnp.float32)
    grad_total, attended_all = lax.scan(group_step, initial, (moved, segment, upstream_all))
    attended = attended_all.transpose(0, 2, 1, 3).reshape(N_DP * group_rows, HEADS * DH)
    grad_w = grad_total.transpose(1, 0, 2).reshape(D, HEADS * 3 * DH)
    return (attended, grad_w)
```

```python
import math

import jax
import jax.numpy as jnp
from jax import lax
from jax.experimental import pallas as pl
from jax.experimental.pallas import tpu as pltpu
from jax.sharding import PartitionSpec as P

EPSILON = 1e-06
MESH = pl.DeviceIdType.MESH
F32 = jnp.float32
BF16 = jnp.bfloat16
D = 2560
DH = 128
RB = 128
NC = 16
NG = 16
GR = NC * RB
CHUNKS = 5
CW = D // CHUNKS
PW = CW // 2
HALF = RB // 2
QUART = HALF // 2
SHARD = D // NG
TN = (((0,), (0,)), ((), ()))
NT = (((1,), (1,)), ((), ()))
VMEM_LIMIT = 60 << 20


def aligned(value, step):
    return pl.multiple_of(value, step)


def anchor_of(mv, column, group):
    anchor = group
    for k in range(4):
        anchor = jnp.where(mv[column, 2 * k + 1] == group, mv[column, 2 * k], anchor)
    return anchor


def gather_kernel(
    img, txt, mv, tok, mod, w, cot,
    gout, proj, up,
    modv, sa, sb, sc, sd, se, st2, gath, wfull,
    m1s, m1r, m2s, m2r, gs, gr, wus, wur, wds, wdr, wss, wsr, wl, cs, cr, ls,
):
    dp = lax.axis_index("dp")
    sq = lax.axis_index("seq")
    z, core = dp // 2, dp % 2
    y, x = sq // 4, sq % 4
    st1 = (sa, sb, sc, sd, se)

    barrier = pltpu.get_barrier_semaphore()

    @pl.loop(1, 16)
    def _(k):
        pl.semaphore_signal(
            barrier, inc=1, device_id={"dp": lax.rem(dp + k, 16)}, device_id_type=MESH
        )
        pl.semaphore_signal(
            barrier, inc=1, device_id={"seq": lax.rem(sq + k, 16)}, device_id_type=MESH
        )

    first = sq * RB
    slot = jnp.int32(0)
    start = jnp.int32(0)
    end = jnp.int32(0)
    for i in range(8):
        end = end + img[dp, i]
        hit = first >= end
        slot = slot + hit.astype(jnp.int32)
        start = jnp.where(hit, end, start)
    slot = jnp.minimum(slot, 7)
    limit = txt[dp, slot] - (first - start)

    @pl.loop(0, RB // 16)
    def _(i):
        r0 = aligned(i * 16, 16)
        rows = tok[pl.ds(r0, 16), :].astype(F32)
        centre = jnp.mean(rows, axis=1, keepdims=True)
        offsets = rows - centre
        variance = jnp.mean(offsets * offsets, axis=1, keepdims=True)
        normed = offsets * lax.rsqrt(variance + EPSILON)
        is_text = lax.broadcasted_iota(jnp.int32, (16, 1), 0) + r0 < limit
        shift = jnp.where(is_text, mod[2, pl.ds(slot, 1), :], mod[0, pl.ds(slot, 1), :])
        scale = jnp.where(is_text, mod[3, pl.ds(slot, 1), :], mod[1, pl.ds(slot, 1), :])
        modv[pl.ds(r0, 16), :] = (normed * (1.0 + scale) + shift).astype(BF16)

    pl.semaphore_wait(barrier, 30)

    def cot_copy(h):
        return pltpu.make_async_remote_copy(
            cot.at[:, pl.ds(aligned(h * DH, DH), DH)],
            up.at[pl.ds(aligned(sq * RB, RB), RB), :],
            cs, cr, device_id={"seq": h}, device_id_type=MESH,
        )

    def send_cot():
        pltpu.make_async_copy(
            cot.at[:, pl.ds(aligned(sq * DH, DH), DH)],
            up.at[pl.ds(aligned(sq * RB, RB), RB), :],
            cr,
        ).start()

        @pl.loop(1, 16)
        def _(k):
            cot_copy(lax.rem(sq + k, 16)).start()

    def send_m1(t):
        def piece(d):
            return modv.at[
                pl.ds(aligned(d // 2 * 16, 16), 16),
                pl.ds(aligned(t * CW + d % 2 * PW, PW), PW),
            ]

        pltpu.make_async_copy(piece(dp), st1[t].at[dp], m1r.at[t]).start()

        @pl.loop(1, 16)
        def _(k):
            d = lax.rem(dp + k, 16)
            pltpu.make_async_remote_copy(
                piece(d), st1[t].at[dp], m1s.at[t], m1r.at[t],
                device_id={"dp": d}, device_id_type=MESH,
            ).start()

    def send_m2(t):
        pltpu.make_async_copy(st1[t], st1[t], m1r.at[t]).wait()

        @pl.loop(0, 16)
        def _(d):
            st2[t, d] = st1[t][anchor_of(mv, sq, d)]

        place = gath.at[
            pl.ds(aligned(sq * RB + dp // 2 * 16, 16), 16),
            pl.ds(aligned(t * CW + dp % 2 * PW, PW), PW),
        ]
        pltpu.make_async_copy(st2.at[t, dp], place, m2r.at[t]).start()

        @pl.loop(1, 16)
        def _(k):
            d = lax.rem(dp + k, 16)
            pltpu.make_async_remote_copy(
                st2.at[t, d], place, m2s.at[t], m2r.at[t],
                device_id={"dp": d}, device_id_type=MESH,
            ).start()

    def column(h, i, j):
        if h == 0:
            return lax.rem(y + j + 4, 4) * 4 + lax.rem(x + i + 4, 4)
        return lax.rem(y + i + 4, 4) * 4 + lax.rem(x + j + 4, 4)

    def beside(along_x, step):
        if along_x:
            return {"seq": y * 4 + lax.rem(x + step + 4, 4)}
        return {"seq": lax.rem(y + step + 4, 4) * 4 + x}

    def region(t, h, i, j, part):
        low = column(h, i, j) * RB + h * HALF + (QUART if part == 2 else 0)
        count = HALF if part == 0 else QUART
        return gath.at[pl.ds(aligned(low, QUART), count), pl.ds(t * CW, CW)]

    offsets = (0, -1, 1, 2)

    def event(t, h, e):
        if e < 4:
            along_x = h == 0
            i, j = {0: (0, 0), 1: (0, 0), 2: (-1, 0), 3: (1, 0)}[e]
            gi, gj = {0: (-1, 0), 1: (1, 0), 2: (2, 0), 3: (2, 0)}[e]
            kind = e
        else:
            along_x = h == 1
            k, kind = (e - 4) // 4, (e - 4) % 4
            o = offsets[k]
            i, j = o, {0: 0, 1: 0, 2: -1, 3: 1}[kind]
            gi, gj = o, {0: -1, 1: 1, 2: 2, 3: 2}[kind]
        part = {0: 0, 1: 0, 2: 1, 3: 2}[kind]
        step = 1 if kind in (0, 2) else -1
        return (i, j, gi, gj, part, along_x, step)

    def put(t, h, e):
        i, j, _, _, part, along_x, step = event(t, h, e)
        place = region(t, h, i, j, part)
        pltpu.make_async_remote_copy(
            place, place, gs.at[t, h, e], gr.at[t, h, e],
            device_id=beside(along_x, step), device_id_type=MESH,
        ).start()

    def got(t, h, e):
        _, _, gi, gj, part, _, _ = event(t, h, e)
        place = region(t, h, gi, gj, part)
        pltpu.make_async_copy(place, place, gr.at[t, h, e]).wait()

    def sent(t, h, e):
        i, j, _, _, part, _, _ = event(t, h, e)
        place = region(t, h, i, j, part)
        pltpu.make_async_copy(place, place, gs.at[t, h, e]).wait()

    def stage2(t):
        place = gath.at[pl.ds(aligned(sq * RB, RB), RB), pl.ds(t * CW, CW)]
        pltpu.make_async_copy(place, place, m2r.at[t]).wait()
        for e in (0, 1, 4, 5):
            for h in (0, 1):
                put(t, h, e)

    def stage3(t):
        for h in (0, 1):
            got(t, h, 0)
            for e in (2, 8, 9):
                put(t, h, e)
        for h in (0, 1):
            got(t, h, 1)
            for e in (3, 12, 13):
                put(t, h, e)
        for h in (0, 1):
            for kind in (0, 1):
                got(t, h, 4 + kind)
                put(t, h, 6 + kind)

    def stage4(t):
        for h in (0, 1):
            got(t, h, 2)
            got(t, h, 3)
            for e in (16, 17):
                put(t, h, e)
        for k in (1, 2):
            for h in (0, 1):
                for kind in (0, 1):
                    got(t, h, 4 + 4 * k + kind)
                    put(t, h, 6 + 4 * k + kind)

    def stage5(t):
        for h in (0, 1):
            for kind in (0, 1):
                got(t, h, 16 + kind)
                put(t, h, 18 + kind)

    def stage6(t):
        for h in (0, 1):
            for k in range(4):
                got(t, h, 6 + 4 * k)
                got(t, h, 7 + 4 * k)
        pltpu.make_async_copy(
            gath.at[:, pl.ds(t * CW, CW)], gout.at[:, pl.ds(t * CW, CW)], ls.at[t]
        ).start()

        @pl.loop(0, GR // 256)
        def _(i):
            r0 = aligned(i * 256, 256)
            term = jnp.dot(
                gath[pl.ds(r0, 256), pl.ds(t * CW, CW)],
                wfull[pl.ds(t * CW, CW), :],
                preferred_element_type=F32,
            )
            if t == 0:
                proj[pl.ds(r0, 256), :] = term
            else:
                proj[pl.ds(r0, 256), :] += term

    def shard(dz, c):
        return wfull.at[pl.ds(aligned((lax.rem(z + dz + 8, 8) * 2 + c) * SHARD, 16), SHARD), :]

    def to_z(step):
        return {"dp": lax.rem(z + step + 8, 8) * 2 + core}

    def w_put(src, dst, ssem, rsem, device):
        pltpu.make_async_remote_copy(
            src, dst, ssem, rsem, device_id=device, device_id_type=MESH
        ).start()

    def w_got(place, sem):
        pltpu.make_async_copy(place, place, sem).wait()

    other = {"dp": z * 2 + 1 - core}

    def weights(step):
        if step == 0:
            own = shard(0, core)
            pltpu.make_async_copy(w, own, wl).start()
            w_put(w, own, wus.at[0], wur.at[0], to_z(1))
            w_put(w, own, wds.at[0], wdr.at[0], to_z(-1))
            w_put(w, own, wss.at[0], wsr.at[0], other)
            return
        if step <= 4:
            place = shard(-step, core)
            w_got(place, wur.at[step - 1])
            if step < 4:
                w_put(place, place, wus.at[step], wur.at[step], to_z(1))
            w_put(place, place, wss.at[step], wsr.at[step], other)
        if step <= 3:
            place = shard(step, core)
            w_got(place, wdr.at[step - 1])
            if step < 3:
                w_put(place, place, wds.at[step], wdr.at[step], to_z(-1))
            w_put(place, place, wss.at[4 + step], wsr.at[4 + step], other)

    sib_order = (0, -1, -2, -3, -4, 1, 2, 3)

    def weights_end():
        w_got(shard(0, core), wl)
        for k in range(8):
            w_got(shard(sib_order[k], 1 - core), wsr.at[k])

    send_m1(0)
    send_cot()
    send_m1(1)
    stages = ((5, stage5), (4, stage4), (3, stage3), (2, stage2))
    for n in range(CHUNKS + 5):
        for s, run in stages:
            t = n - s + 1
            if 0 <= t < CHUNKS:
                run(t)
        if n < CHUNKS:
            send_m2(n)
        if n + 2 < CHUNKS:
            send_m1(n + 2)
        if n <= 4:
            weights(n)
        if n == 5:
            weights_end()
        t = n - 5
        if 0 <= t < CHUNKS:
            stage6(t)

    pltpu.make_async_copy(up, up, cr).wait()
    part = up.at[pl.ds(0, 15 * RB), :]
    pltpu.make_async_copy(part, part, cs).wait()
    for t in range(CHUNKS):
        part = st1[t].at[pl.ds(0, 15)]
        pltpu.make_async_copy(part, part, m1s.at[t]).wait()
        pltpu.make_async_copy(part, part, m2s.at[t]).wait()
        for h in (0, 1):
            for e in range(20):
                sent(t, h, e)
        pltpu.make_async_copy(
            gath.at[:, pl.ds(t * CW, CW)], gout.at[:, pl.ds(t * CW, CW)], ls.at[t]
        ).wait()
    own = shard(0, core)
    for k in range(4):
        w_got(own, wus.at[k])
    for k in range(3):
        w_got(own, wds.at[k])
    for k in range(8):
        w_got(own, wss.at[k])


def gather_call(img, txt, mv, tok, mod, w, cot):
    vmem = pl.BlockSpec(memory_space=pltpu.VMEM)
    smem = pl.BlockSpec(memory_space=pltpu.SMEM)
    hbm = pl.BlockSpec(memory_space=pl.ANY)
    dma = pltpu.SemaphoreType.DMA
    return pl.pallas_call(
        gather_kernel,
        name="gather_project",
        out_shape=(
            jax.ShapeDtypeStruct((GR, D), BF16),
            jax.ShapeDtypeStruct((GR, 3 * DH), F32),
            jax.ShapeDtypeStruct((GR, DH), BF16),
        ),
        in_specs=[smem, smem, smem, vmem, vmem, hbm, hbm],
        out_specs=(hbm, vmem, hbm),
        scratch_shapes=[
            pltpu.VMEM((RB, D), BF16),
            *[pltpu.VMEM((16, 16, PW), BF16)] * CHUNKS,
            pltpu.VMEM((CHUNKS, 16, 16, PW), BF16),
            pltpu.VMEM((GR, D), BF16),
            pltpu.VMEM((D, 3 * DH), BF16),
            dma((CHUNKS,)), dma((CHUNKS,)), dma((CHUNKS,)), dma((CHUNKS,)),
            dma((CHUNKS, 2, 20)), dma((CHUNKS, 2, 20)),
            dma((4,)), dma((4,)), dma((3,)), dma((3,)), dma((8,)), dma((8,)), dma(()),
            dma(()), dma(()), dma((CHUNKS,)),
        ],
        compiler_params=pltpu.CompilerParams(
            collective_id=0, has_side_effects=True, vmem_limit_bytes=VMEM_LIMIT
        ),
    )(img, txt, mv, tok, mod, w, cot)


MASK = 4096.0


def attention_kernel(
    img, mv, proj, up, gain,
    att, hg,
    qx, kx, vx, ux, us, es, dq, dk, dv, place, back, low, high,
):
    group = lax.axis_index("dp")
    scale = 1.0 / math.sqrt(DH)
    segs = []
    for c in range(NC):
        anchor = anchor_of(mv, c, group)
        slot = jnp.int32(0)
        end = jnp.int32(0)
        for i in range(8):
            end = end + img[anchor, i]
            slot = slot + (c * RB >= end).astype(jnp.int32)
        segs.append(anchor * 8 + slot)
    for c in range(NC):
        less = jnp.int32(0)
        same = jnp.int32(0)
        ahead = jnp.int32(0)
        for o in range(NC):
            less = less + (segs[o] < segs[c]).astype(jnp.int32)
            equal = (segs[o] == segs[c]).astype(jnp.int32)
            same = same + equal
            if o < c:
                ahead = ahead + equal
        spot = less + ahead
        place[c] = spot
        back[spot] = c
        low[spot] = less
        high[spot] = less + same

    lanes = lax.broadcasted_iota(jnp.int32, (RB, DH), 1)
    gain_q = gain[0:1, :]
    gain_k = gain[1:2, :]

    @pl.loop(0, NC)
    def _(c):
        r0 = aligned(c * RB, RB)
        spot = place[c]
        s0 = aligned(spot * RB, RB)
        mark = low[spot]
        q = proj[pl.ds(r0, RB), 0:DH]
        k = proj[pl.ds(r0, RB), DH : 2 * DH]
        qi = lax.rsqrt(jnp.mean(q * q, axis=1, keepdims=True) + EPSILON)
        ki = lax.rsqrt(jnp.mean(k * k, axis=1, keepdims=True) + EPSILON)
        qx[pl.ds(s0, RB), 0:DH] = (q * qi * gain_q).astype(BF16)
        kx[pl.ds(s0, RB), 0:DH] = (k * ki * gain_k).astype(BF16)
        vx[pl.ds(s0, RB), 0:DH] = proj[pl.ds(r0, RB), 2 * DH : 3 * DH].astype(BF16)
        hot = lanes == mark
        tail = lanes == NC
        qx[pl.ds(s0, RB), DH:] = jnp.where(hot, MASK, jnp.where(tail, 1.0, 0.0)).astype(BF16)
        kx[pl.ds(s0, RB), DH:] = jnp.where(hot, 1.0, jnp.where(tail, -MASK, 0.0)).astype(BF16)
        vx[pl.ds(s0, RB), DH:] = jnp.where(lanes < 2, -1.0, 0.0).astype(BF16)
        us[pl.ds(s0, RB), :] = up[pl.ds(r0, RB), :]

    dk[...] = jnp.zeros_like(dk)
    dv[...] = jnp.zeros_like(dv)
    wide = lax.broadcasted_iota(jnp.int32, (2 * RB, DH), 1)
    factor = scale * math.log2(math.e)

    @pl.loop(0, NC // 2)
    def _(qt):
        q0 = aligned(qt * 2 * RB, 2 * RB)
        first = low[2 * qt] // 2
        last = (high[2 * qt + 1] + 1) // 2
        q_tile = qx[pl.ds(q0, 2 * RB), :]

        def forward(kt, total):
            k0 = aligned(kt * 2 * RB, 2 * RB)
            scores = lax.dot_general(
                q_tile, kx[pl.ds(k0, 2 * RB), :], NT, preferred_element_type=F32
            )
            e = jnp.exp2(scores * factor).astype(BF16)
            es[kt] = e
            return total + jnp.dot(e, vx[pl.ds(k0, 2 * RB), :], preferred_element_type=F32)

        total = lax.fori_loop(first, last, forward, jnp.zeros((2 * RB, 2 * DH), F32))
        inverse = -1.0 / total[:, DH : DH + 1]
        out = (total[:, :DH] * inverse).astype(BF16)
        for b in range(2):
            att[pl.ds(aligned(back[2 * qt + b] * RB, RB), RB), :] = out[b * RB : (b + 1) * RB]
        u = us[pl.ds(q0, 2 * RB), :].astype(F32)
        delta = jnp.sum(u * out.astype(F32), axis=1, keepdims=True) * inverse
        coarse = delta.astype(BF16).astype(F32)
        fine = delta - coarse
        u_tile = (u * inverse).astype(BF16)
        ux[:, :DH] = u_tile
        ux[:, DH:] = jnp.where(wide == 0, coarse, jnp.where(wide == 1, fine, 0.0)).astype(BF16)

        def backward(kt, grad):
            k0 = aligned(kt * 2 * RB, 2 * RB)
            e = es[kt]
            inner = lax.dot_general(
                ux[...], vx[pl.ds(k0, 2 * RB), :], NT, preferred_element_type=F32
            )
            ds = (e.astype(F32) * inner).astype(BF16)
            dv[pl.ds(k0, 2 * RB), :] += lax.dot_general(
                e, ux[:, :DH], TN, preferred_element_type=F32
            )
            dk[pl.ds(k0, 2 * RB), :] += lax.dot_general(
                ds, qx[pl.ds(q0, 2 * RB), :DH], TN, preferred_element_type=F32
            )
            return grad + jnp.dot(ds, kx[pl.ds(k0, 2 * RB), :DH], preferred_element_type=F32)

        dq[pl.ds(q0, 2 * RB), :] = lax.fori_loop(
            first, last, backward, jnp.zeros((2 * RB, DH), F32)
        )

    @pl.loop(0, NC)
    def _(c):
        r0 = aligned(c * RB, RB)
        s0 = aligned(place[c] * RB, RB)

        def back_norm(values, gains, upstream):
            inverse = lax.rsqrt(jnp.mean(values * values, axis=1, keepdims=True) + EPSILON)
            scaled = upstream * gains
            inner = jnp.mean(scaled * values, axis=1, keepdims=True)
            return inverse * scaled - values * (inverse * inverse * inverse * inner)

        q = proj[pl.ds(r0, RB), 0:DH]
        k = proj[pl.ds(r0, RB), DH : 2 * DH]
        hg[pl.ds(r0, RB), 0:DH] = back_norm(q, gain_q, dq[pl.ds(s0, RB), :] * scale).astype(BF16)
        hg[pl.ds(r0, RB), DH : 2 * DH] = back_norm(
            k, gain_k, dk[pl.ds(s0, RB), :] * scale
        ).astype(BF16)
        hg[pl.ds(r0, RB), 2 * DH :] = dv[pl.ds(s0, RB), :].astype(BF16)


def attention_call(img, mv, proj, up, gain):
    vmem = pl.BlockSpec(memory_space=pltpu.VMEM)
    smem = pl.BlockSpec(memory_space=pltpu.SMEM)
    return pl.pallas_call(
        attention_kernel,
        name="attention",
        out_shape=(
            jax.ShapeDtypeStruct((GR, DH), BF16),
            jax.ShapeDtypeStruct((GR, 3 * DH), BF16),
        ),
        in_specs=[smem, smem, vmem, vmem, vmem],
        out_specs=(vmem, vmem),
        scratch_shapes=[
            pltpu.VMEM((GR, 2 * DH), BF16),
            pltpu.VMEM((GR, 2 * DH), BF16),
            pltpu.VMEM((GR, 2 * DH), BF16),
            pltpu.VMEM((2 * RB, 2 * DH), BF16),
            pltpu.VMEM((GR, DH), BF16),
            pltpu.VMEM((NC // 2, 2 * RB, 2 * RB), BF16),
            pltpu.VMEM((GR, DH), F32),
            pltpu.VMEM((GR, DH), F32),
            pltpu.VMEM((GR, DH), F32),
            pltpu.SMEM((NC,), jnp.int32),
            pltpu.SMEM((NC,), jnp.int32),
            pltpu.SMEM((NC,), jnp.int32),
            pltpu.SMEM((NC,), jnp.int32),
        ],
        compiler_params=pltpu.CompilerParams(vmem_limit_bytes=VMEM_LIMIT),
    )(img, mv, proj, up, gain)


STEPS = (2, 3, 1, 0)
FC = 4 * SHARD


def reduce_kernel(
    rows, hg, grad,
    xs, dw, pair, su, ru, sd, rd,
    xsem, ps, pr, us, ur, ds, dr,
):
    dp = lax.axis_index("dp")
    z, core = dp // 2, dp % 2
    other = {"dp": z * 2 + 1 - core}

    def to_z(step):
        return {"dp": lax.rem(z + step + 8, 8) * 2 + core}

    def chunk(n):
        return lax.rem(z // 2 + STEPS[n], 4)

    def load(n):
        return pltpu.make_async_copy(
            rows.at[:, pl.ds(aligned(chunk(n) * FC, 128), FC)], xs.at[n], xsem.at[n]
        )

    for n in range(4):
        load(n).start()
    barrier = pltpu.get_barrier_semaphore()
    for device in (other, to_z(1), to_z(-1)):
        pl.semaphore_signal(barrier, inc=1, device_id=device, device_id_type=MESH)

    def compute(n):
        load(n).wait()
        m = chunk(n)
        dw[m] = lax.dot_general(xs[n], hg[...], TN, preferred_element_type=F32)

    def pair_copy(n, j):
        m = chunk(n)
        return pltpu.make_async_remote_copy(
            dw.at[m, pl.ds(aligned((2 * j + 1 - core) * SHARD, 16), SHARD), :],
            pair.at[2 * m + j],
            ps.at[n, j], pr.at[n, j], device_id=other, device_id_type=MESH,
        )

    def pair_send(n):
        for j in range(2):
            pair_copy(n, j).start()

    def pair_wait(n):
        for j in range(2):
            pair_copy(n, j).wait_recv()

    def part(dz):
        zz = lax.rem(z + dz + 8, 8)
        at = aligned((lax.rem(zz, 2) * 2 + core) * SHARD, 16)
        return dw[zz // 2, pl.ds(at, SHARD), :] + pair[zz]

    def up_copy(k):
        return pltpu.make_async_remote_copy(
            su.at[k], ru.at[k], us.at[k], ur.at[k], device_id=to_z(1), device_id_type=MESH
        )

    def down_copy(k):
        return pltpu.make_async_remote_copy(
            sd.at[k], rd.at[k], ds.at[k], dr.at[k], device_id=to_z(-1), device_id_type=MESH
        )

    def go_up(k):
        value = part(4 - k)
        if k:
            up_copy(k - 1).wait_recv()
            value = value + ru[k - 1].astype(F32)
        su[k] = value.astype(BF16)
        up_copy(k).start()

    def go_down(k):
        value = part(k - 3)
        if k:
            down_copy(k - 1).wait_recv()
            value = value + rd[k - 1].astype(F32)
        sd[k] = value.astype(BF16)
        down_copy(k).start()

    compute(0)
    pl.semaphore_wait(barrier, 3)
    pair_send(0)
    compute(1)
    pair_send(1)
    pair_wait(0)
    go_up(0)
    compute(2)
    pair_send(2)
    pair_wait(1)
    go_down(0)
    compute(3)
    pair_send(3)
    pair_wait(2)
    go_up(1)
    go_down(1)
    go_up(2)
    pair_wait(3)
    go_down(2)
    go_up(3)
    total = part(0)
    down_copy(2).wait_recv()
    total = total + rd[2].astype(F32)
    up_copy(3).wait_recv()
    grad[...] = total + ru[3].astype(F32)
    for n in range(4):
        for j in range(2):
            pair_copy(n, j).wait_send()
    for k in range(4):
        up_copy(k).wait_send()
    for k in range(3):
        down_copy(k).wait_send()


def reduce_call(rows, hg):
    vmem = pl.BlockSpec(memory_space=pltpu.VMEM)
    hbm = pl.BlockSpec(memory_space=pl.ANY)
    dma = pltpu.SemaphoreType.DMA
    wide = 3 * DH
    return pl.pallas_call(
        reduce_kernel,
        name="grad_reduce",
        out_shape=jax.ShapeDtypeStruct((SHARD, wide), F32),
        in_specs=[hbm, vmem],
        out_specs=vmem,
        scratch_shapes=[
            pltpu.VMEM((4, GR, FC), BF16),
            pltpu.VMEM((4, FC, wide), F32),
            pltpu.VMEM((8, SHARD, wide), F32),
            pltpu.VMEM((4, SHARD, wide), BF16),
            pltpu.VMEM((4, SHARD, wide), BF16),
            pltpu.VMEM((3, SHARD, wide), BF16),
            pltpu.VMEM((3, SHARD, wide), BF16),
            dma((4,)), dma((4, 2)), dma((4, 2)), dma((4,)), dma((4,)), dma((3,)), dma((3,)),
        ],
        compiler_params=pltpu.CompilerParams(
            collective_id=1, has_side_effects=True, vmem_limit_bytes=VMEM_LIMIT
        ),
    )(rows, hg)


def body(tokens, modulation, img_size, text_count, move_list, w_qkv, qk_gain, cotangent):
    moves = move_list.reshape(NC, 8)
    gathered, projected, upstream = gather_call(
        img_size, text_count, moves, tokens, modulation, w_qkv, cotangent
    )
    attended, head_grads = attention_call(img_size, moves, projected, upstream, qk_gain)
    return (attended, reduce_call(gathered, head_grads))


def solution(mesh):
    placed = (
        P(("dp", "seq"), None),
        P(None, "dp", None),
        P(),
        P(),
        P(),
        P("dp", "seq"),
        P(None, "seq"),
        P(("dp", "seq"), None),
    )
    return jax.shard_map(
        body,
        mesh=mesh,
        in_specs=placed,
        out_specs=(P("dp", "seq"), P("dp", "seq")),
        check_vma=False,
    )
```

```python
import math

import jax
import jax.numpy as jnp
from jax import lax
from jax.experimental import pallas as pl
from jax.experimental.pallas import tpu as pltpu
from jax.sharding import PartitionSpec as P

EPSILON = 1e-06
MESH = pl.DeviceIdType.MESH
F32 = jnp.float32
BF16 = jnp.bfloat16
D = 2560
DH = 128
RB = 128
NC = 16
NG = 16
GR = NC * RB
CHUNKS = 5
CW = D // CHUNKS
PW = CW // 2
HALF = RB // 2
QUART = HALF // 2
SHARD = D // NG
LAST = (6, 7, 10, 11, 14, 15, 18, 19)
TN = (((0,), (0,)), ((), ()))
NT = (((1,), (1,)), ((), ()))
VMEM_LIMIT = 60 << 20


def aligned(value, step):
    return pl.multiple_of(value, step)


def anchor_of(mv, column, group):
    anchor = group
    for k in range(4):
        anchor = jnp.where(mv[k, 1, column] == group, mv[k, 0, column], anchor)
    return anchor


def gather_kernel(
    img, txt, mv, tok, mod, w, cot,
    gout, proj, up,
    modv, *scratch,
):
    st1 = scratch[:CHUNKS]
    st2, gath, wfull, m1s, m1r, m2s, m2r, gs, gr, gf, *scratch = scratch[CHUNKS:]
    wus, wur, wds, wdr, wss, wsr, wl, cs, cr, ls = scratch
    dp = lax.axis_index("dp")
    sq = lax.axis_index("seq")
    z, core = dp // 2, dp % 2
    y, x = sq // 4, sq % 4

    barrier = pltpu.get_barrier_semaphore()

    groups = [lax.rem(dp + k, 16) for k in range(16)]
    columns = [lax.rem(sq + k, 16) for k in range(16)]
    for k in range(1, 16):
        pl.semaphore_signal(
            barrier, inc=1, device_id={"dp": groups[k]}, device_id_type=MESH
        )
        pl.semaphore_signal(
            barrier, inc=1, device_id={"seq": columns[k]}, device_id_type=MESH
        )
    piece_rows = [aligned(d // 2 * 16, 16) for d in groups]
    piece_cols = [aligned(lax.rem(d, 2) * PW, PW) for d in groups]
    ys = [lax.rem(y + k, 4) for k in range(4)]
    xs = [lax.rem(x + k, 4) for k in range(4)]
    bases = [[(ys[j] * 4 + xs[i]) * RB for i in range(4)] for j in range(4)]
    anchors = [anchor_of(mv, sq, d) for d in range(16)]

    first = sq * RB
    slot = jnp.int32(0)
    start = jnp.int32(0)
    end = jnp.int32(0)
    for i in range(8):
        end = end + img[i, dp]
        hit = first >= end
        slot = slot + hit.astype(jnp.int32)
        start = jnp.where(hit, end, start)
    slot = jnp.minimum(slot, 7)
    limit = txt[slot, dp] - (first - start)

    @pl.loop(0, RB // 16)
    def _(i):
        r0 = aligned(i * 16, 16)
        rows = tok[pl.ds(r0, 16), :].astype(F32)
        centre = jnp.mean(rows, axis=1, keepdims=True)
        offsets = rows - centre
        variance = jnp.mean(offsets * offsets, axis=1, keepdims=True)
        normed = offsets * lax.rsqrt(variance + EPSILON)
        is_text = lax.broadcasted_iota(jnp.int32, (16, 1), 0) + r0 < limit
        shift = jnp.where(is_text, mod[2, pl.ds(slot, 1), :], mod[0, pl.ds(slot, 1), :])
        scale = jnp.where(is_text, mod[3, pl.ds(slot, 1), :], mod[1, pl.ds(slot, 1), :])
        modv[pl.ds(r0, 16), :] = (normed * (1.0 + scale) + shift).astype(BF16)

    pl.semaphore_wait(barrier, 30)

    def cot_copy(h):
        return pltpu.make_async_remote_copy(
            cot.at[:, pl.ds(aligned(h * DH, DH), DH)],
            up.at[pl.ds(aligned(sq * RB, RB), RB), :],
            cs, cr, device_id={"seq": h}, device_id_type=MESH,
        )

    def send_cot():
        pltpu.make_async_copy(
            cot.at[:, pl.ds(aligned(sq * DH, DH), DH)],
            up.at[pl.ds(aligned(sq * RB, RB), RB), :],
            cr,
        ).start()

        for k in range(1, 16):
            cot_copy(columns[k]).start()

    def send_m1(t):
        for k in range(16):
            piece = modv.at[pl.ds(piece_rows[k], 16), pl.ds(t * CW + piece_cols[k], PW)]
            if k == 0:
                pltpu.make_async_copy(piece, st1[t].at[dp], m1r.at[t]).start()
            else:
                pltpu.make_async_remote_copy(
                    piece, st1[t].at[dp], m1s.at[t], m1r.at[t],
                    device_id={"dp": groups[k]}, device_id_type=MESH,
                ).start()

    def send_m2(t):
        pltpu.make_async_copy(st1[t], st1[t], m1r.at[t]).wait()
        for d in range(16):
            st2[t, d] = st1[t][anchors[d]]
        place = gath.at[
            pl.ds(aligned(sq * RB + piece_rows[0], 16), 16), pl.ds(t * CW + piece_cols[0], PW)
        ]
        pltpu.make_async_copy(st2.at[t, dp], place, m2r.at[t]).start()
        for k in range(1, 16):
            pltpu.make_async_remote_copy(
                st2.at[t, groups[k]], place, m2s.at[t], m2r.at[t],
                device_id={"dp": groups[k]}, device_id_type=MESH,
            ).start()

    def base(h, i, j):
        if h == 0:
            return bases[j % 4][i % 4]
        return bases[i % 4][j % 4]

    def beside(along_x, step):
        if along_x:
            return {"seq": ys[0] * 4 + xs[step % 4]}
        return {"seq": ys[step % 4] * 4 + xs[0]}

    def region(t, h, i, j, part):
        low = base(h, i, j) + h * HALF + (QUART if part == 2 else 0)
        count = HALF if part == 0 else QUART
        return gath.at[pl.ds(aligned(low, QUART), count), pl.ds(t * CW, CW)]

    offsets = (0, -1, 1, 2)

    def event(t, h, e):
        if e < 4:
            along_x = h == 0
            i, j = {0: (0, 0), 1: (0, 0), 2: (-1, 0), 3: (1, 0)}[e]
            gi, gj = {0: (-1, 0), 1: (1, 0), 2: (2, 0), 3: (2, 0)}[e]
            kind = e
        else:
            along_x = h == 1
            k, kind = (e - 4) // 4, (e - 4) % 4
            o = offsets[k]
            i, j = o, {0: 0, 1: 0, 2: -1, 3: 1}[kind]
            gi, gj = o, {0: -1, 1: 1, 2: 2, 3: 2}[kind]
        part = {0: 0, 1: 0, 2: 1, 3: 2}[kind]
        step = 1 if kind in (0, 2) else -1
        return (i, j, gi, gj, part, along_x, step)

    def put(t, h, e):
        i, j, _, _, part, along_x, step = event(t, h, e)
        place = region(t, h, i, j, part)
        pltpu.make_async_remote_copy(
            place, place, gs.at[t], gf.at[t] if e in LAST else gr.at[t, h, e],
            device_id=beside(along_x, step), device_id_type=MESH,
        ).start()

    def got(t, h, e):
        _, _, gi, gj, part, _, _ = event(t, h, e)
        place = region(t, h, gi, gj, part)
        pltpu.make_async_copy(place, place, gr.at[t, h, e]).wait()

    def stage2(t):
        place = gath.at[pl.ds(aligned(sq * RB, RB), RB), pl.ds(t * CW, CW)]
        pltpu.make_async_copy(place, place, m2r.at[t]).wait()
        for e in (0, 1, 4, 5):
            for h in (0, 1):
                put(t, h, e)

    def stage3(t):
        for h in (0, 1):
            got(t, h, 0)
            for e in (2, 8, 9):
                put(t, h, e)
        for h in (0, 1):
            got(t, h, 1)
            for e in (3, 12, 13):
                put(t, h, e)
        for h in (0, 1):
            for kind in (0, 1):
                got(t, h, 4 + kind)
                put(t, h, 6 + kind)

    def stage4(t):
        for h in (0, 1):
            got(t, h, 2)
            got(t, h, 3)
            for e in (16, 17):
                put(t, h, e)
        for k in (1, 2):
            for h in (0, 1):
                for kind in (0, 1):
                    got(t, h, 4 + 4 * k + kind)
                    put(t, h, 6 + 4 * k + kind)

    def stage5(t):
        for h in (0, 1):
            for kind in (0, 1):
                got(t, h, 16 + kind)
                put(t, h, 18 + kind)

    def stage6(t):
        place = gath.at[pl.ds(0, 16 * QUART), pl.ds(t * CW, CW)]
        pltpu.make_async_copy(place, place, gf.at[t]).wait()
        pltpu.make_async_copy(
            gath.at[:, pl.ds(t * CW, CW)], gout.at[:, pl.ds(t * CW, CW)], ls.at[t]
        ).start()

        @pl.loop(0, GR // 256)
        def _(i):
            r0 = aligned(i * 256, 256)
            term = jnp.dot(
                gath[pl.ds(r0, 256), pl.ds(t * CW, CW)],
                wfull[pl.ds(t * CW, CW), :],
                preferred_element_type=F32,
            )
            if t == 0:
                proj[pl.ds(r0, 256), :] = term
            else:
                proj[pl.ds(r0, 256), :] += term

    def shard(dz, c):
        return wfull.at[pl.ds(aligned((lax.rem(z + dz + 8, 8) * 2 + c) * SHARD, 16), SHARD), :]

    def to_z(step):
        return {"dp": lax.rem(z + step + 8, 8) * 2 + core}

    def w_put(src, dst, ssem, rsem, device):
        pltpu.make_async_remote_copy(
            src, dst, ssem, rsem, device_id=device, device_id_type=MESH
        ).start()

    def w_got(place, sem):
        pltpu.make_async_copy(place, place, sem).wait()

    other = {"dp": z * 2 + 1 - core}

    def weights(step):
        if step == 0:
            own = shard(0, core)
            pltpu.make_async_copy(w, own, wl).start()
            w_put(w, own, wus.at[0], wur.at[0], to_z(1))
            w_put(w, own, wds.at[0], wdr.at[0], to_z(-1))
            w_put(w, own, wss.at[0], wsr.at[0], other)
            return
        if step <= 4:
            place = shard(-step, core)
            w_got(place, wur.at[step - 1])
            if step < 4:
                w_put(place, place, wus.at[step], wur.at[step], to_z(1))
            w_put(place, place, wss.at[step], wsr.at[step], other)
        if step <= 3:
            place = shard(step, core)
            w_got(place, wdr.at[step - 1])
            if step < 3:
                w_put(place, place, wds.at[step], wdr.at[step], to_z(-1))
            w_put(place, place, wss.at[4 + step], wsr.at[4 + step], other)

    sib_order = (0, -1, -2, -3, -4, 1, 2, 3)

    def weights_end():
        w_got(shard(0, core), wl)
        for k in range(8):
            w_got(shard(sib_order[k], 1 - core), wsr.at[k])

    send_m1(0)
    send_cot()
    stages = ((5, stage5), (4, stage4), (3, stage3), (2, stage2))
    for n in range(CHUNKS + 5):
        for s, run in stages:
            t = n - s + 1
            if 0 <= t < CHUNKS:
                run(t)
        if n < CHUNKS:
            send_m2(n)
        if n == 0:
            send_m1(1)
        if n + 2 < CHUNKS:
            send_m1(n + 2)
        if n <= 4:
            weights(n)
        if n == 5:
            weights_end()
        if 0 <= n - 5 < CHUNKS:
            stage6(n - 5)

    pltpu.make_async_copy(up, up, cr).wait()
    part = up.at[pl.ds(0, 15 * RB), :]
    pltpu.make_async_copy(part, part, cs).wait()
    for t in range(CHUNKS):
        part = st1[t].at[pl.ds(0, 15)]
        pltpu.make_async_copy(part, part, m1s.at[t]).wait()
        pltpu.make_async_copy(part, part, m2s.at[t]).wait()
        part = gath.at[pl.ds(0, 20 * (HALF + QUART)), pl.ds(t * CW, CW)]
        pltpu.make_async_copy(part, part, gs.at[t]).wait()
        pltpu.make_async_copy(
            gath.at[:, pl.ds(t * CW, CW)], gout.at[:, pl.ds(t * CW, CW)], ls.at[t]
        ).wait()
    own = shard(0, core)
    for k in range(4):
        w_got(own, wus.at[k])
    for k in range(3):
        w_got(own, wds.at[k])
    for k in range(8):
        w_got(own, wss.at[k])


def gather_call(img, txt, mv, tok, mod, w, cot):
    vmem = pl.BlockSpec(memory_space=pltpu.VMEM)
    smem = pl.BlockSpec(memory_space=pltpu.SMEM)
    hbm = pl.BlockSpec(memory_space=pl.ANY)
    dma = pltpu.SemaphoreType.DMA
    return pl.pallas_call(
        gather_kernel,
        name="gather_project",
        out_shape=(
            jax.ShapeDtypeStruct((GR, D), BF16),
            jax.ShapeDtypeStruct((GR, 3 * DH), F32),
            jax.ShapeDtypeStruct((GR, DH), BF16),
        ),
        in_specs=[smem, smem, smem, vmem, vmem, hbm, hbm],
        out_specs=(hbm, vmem, hbm),
        scratch_shapes=[
            pltpu.VMEM((RB, D), BF16),
            *[pltpu.VMEM((16, 16, PW), BF16)] * CHUNKS,
            pltpu.VMEM((CHUNKS, 16, 16, PW), BF16),
            pltpu.VMEM((GR, D), BF16),
            pltpu.VMEM((D, 3 * DH), BF16),
            dma((CHUNKS,)), dma((CHUNKS,)), dma((CHUNKS,)), dma((CHUNKS,)),
            dma((CHUNKS,)), dma((CHUNKS, 2, 20)), dma((CHUNKS,)),
            dma((4,)), dma((4,)), dma((3,)), dma((3,)), dma((8,)), dma((8,)), dma(()),
            dma(()), dma(()), dma((CHUNKS,)),
        ],
        compiler_params=pltpu.CompilerParams(
            collective_id=0, has_side_effects=True, vmem_limit_bytes=VMEM_LIMIT
        ),
    )(img, txt, mv, tok, mod, w, cot)


MASK = 4096.0
TQ = 2 * RB
TK = 4 * RB
NQ = GR // TQ
NK = GR // TK
SLOTS = NQ * NK + 6


def attention_kernel(
    img, mv, proj, up, gain,
    att, hg,
    qx, kx, vx, ux, us, es, sa, sb, da, db, oa, dq, dk, dv, place, back, low, high, lq, lk,
):
    group = lax.axis_index("dp")
    scale = 1.0 / math.sqrt(DH)
    segs = []
    for c in range(NC):
        anchor = anchor_of(mv, c, group)
        slot = jnp.int32(0)
        end = jnp.int32(0)
        for i in range(8):
            end = end + img[i, anchor]
            slot = slot + (c * RB >= end).astype(jnp.int32)
        segs.append(anchor * 8 + slot)
    same = [jnp.int32(1)] * NC
    ahead = [jnp.int32(0)] * NC
    for c in range(NC):
        for o in range(c):
            equal = (segs[o] == segs[c]).astype(jnp.int32)
            same[c] = same[c] + equal
            same[o] = same[o] + equal
            ahead[c] = ahead[c] + equal
    keys = [(NC - same[c]) * 256 + segs[c] for c in range(NC)]
    less = [jnp.int32(0)] * NC
    for c in range(NC):
        for o in range(c):
            below = (keys[o] < keys[c]).astype(jnp.int32)
            above = (keys[o] > keys[c]).astype(jnp.int32)
            less[c] = less[c] + below
            less[o] = less[o] + above
    for c in range(NC):
        spot = less[c] + ahead[c]
        place[c] = spot
        back[spot] = c
        low[spot] = less[c]
        high[spot] = less[c] + same[c]

    for i in range(2):
        lq[i] = NQ
        lk[i] = NK

    def list_row(qt, n):
        first = low[qt * (TQ // RB)] // (TK // RB)
        last = (high[qt * (TQ // RB) + TQ // RB - 1] + TK // RB - 1) // (TK // RB)

        def one(kt, n):
            lq[n] = qt
            lk[n] = kt
            return n + 1

        return lax.fori_loop(first, last, one, n)

    count = lax.fori_loop(0, NQ, list_row, jnp.int32(2))
    for i in range(4):
        lq[count + i] = NQ
        lk[count + i] = NK
    steps = (count + 1) // 2

    lanes = lax.broadcasted_iota(jnp.int32, (RB, DH), 1)
    gain_q = gain[0:1, :]
    gain_k = gain[1:2, :]

    @pl.loop(0, NC, unroll=4)
    def _(c):
        r0 = aligned(c * RB, RB)
        spot = place[c]
        s0 = aligned(spot * RB, RB)
        mark = low[spot]
        q = proj[pl.ds(r0, RB), 0:DH]
        k = proj[pl.ds(r0, RB), DH : 2 * DH]
        qi = lax.rsqrt(jnp.mean(q * q, axis=1, keepdims=True) + EPSILON)
        ki = lax.rsqrt(jnp.mean(k * k, axis=1, keepdims=True) + EPSILON)
        qx[pl.ds(s0, RB), 0:DH] = (q * qi * gain_q).astype(BF16)
        kx[pl.ds(s0, RB), 0:DH] = (k * ki * gain_k).astype(BF16)
        vx[pl.ds(s0, RB), 0:DH] = proj[pl.ds(r0, RB), 2 * DH : 3 * DH].astype(BF16)
        hot = lanes == mark
        tail = lanes == NC
        qx[pl.ds(s0, RB), DH:] = jnp.where(hot, MASK, jnp.where(tail, 1.0, 0.0)).astype(BF16)
        kx[pl.ds(s0, RB), DH:] = jnp.where(hot, 1.0, jnp.where(tail, -MASK, 0.0)).astype(BF16)
        vx[pl.ds(s0, RB), DH:] = jnp.full((RB, DH), -1.0, BF16)
        us[pl.ds(s0, RB), :] = up[pl.ds(r0, RB), :]

    oa[...] = jnp.zeros_like(oa)
    dq[...] = jnp.zeros_like(dq)
    dk[...] = jnp.zeros_like(dk)
    dv[...] = jnp.zeros_like(dv)
    factor = scale * math.log2(math.e)

    def rows_q(i):
        return pl.ds(aligned(lq[i] * TQ, TQ), TQ)

    def rows_k(i):
        return pl.ds(aligned(lk[i] * TK, TK), TK)

    def forward(i, mine, other):
        oa[rows_q(i), :] += jnp.dot(es[i], vx[rows_k(i), :], preferred_element_type=F32)
        es[i + 1] = jnp.exp2(other[...] * factor).astype(BF16)
        mine[...] = lax.dot_general(
            qx[rows_q(i + 2), :], kx[rows_k(i + 2), :], NT, preferred_element_type=F32
        )

    @pl.loop(0, steps)
    def _(j):
        forward(2 * j, sa, sb)
        forward(2 * j + 1, sb, sa)

    @pl.loop(0, NC, unroll=4)
    def _(b):
        s0 = aligned(b * RB, RB)
        inverse = -1.0 / oa[pl.ds(s0, RB), DH:]
        out = (oa[pl.ds(s0, RB), :DH] * inverse).astype(BF16)
        att[pl.ds(aligned(back[b] * RB, RB), RB), :] = out
        scaled = us[pl.ds(s0, RB), :].astype(F32) * inverse
        ux[pl.ds(s0, RB), :DH] = scaled.astype(BF16)
        ux[pl.ds(s0, RB), DH:] = (scaled * out.astype(F32)).astype(BF16)

    def backward(i, mine, other, ds_mine, ds_other):
        q_rows = rows_q(i)
        k_rows = rows_k(i)
        dv[k_rows, :] += lax.dot_general(
            es[i], ux[q_rows, :DH], TN, preferred_element_type=F32
        )
        ds = ds_other[...]
        dk[k_rows, :] += lax.dot_general(ds, qx[q_rows, :DH], TN, preferred_element_type=F32)
        dq[q_rows, :] += jnp.dot(ds, kx[k_rows, :DH], preferred_element_type=F32)
        ds_mine[...] = (es[i + 1].astype(F32) * other[...]).astype(BF16)
        mine[...] = lax.dot_general(
            ux[rows_q(i + 2), :], vx[rows_k(i + 2), :], NT, preferred_element_type=F32
        )

    @pl.loop(0, steps)
    def _(j):
        backward(2 * j, sa, sb, da, db)
        backward(2 * j + 1, sb, sa, db, da)

    @pl.loop(0, NC, unroll=4)
    def _(c):
        r0 = aligned(c * RB, RB)
        s0 = aligned(place[c] * RB, RB)

        def back_norm(values, gains, upstream):
            inverse = lax.rsqrt(jnp.mean(values * values, axis=1, keepdims=True) + EPSILON)
            scaled = upstream * gains
            inner = jnp.mean(scaled * values, axis=1, keepdims=True)
            return inverse * scaled - values * (inverse * inverse * inverse * inner)

        q = proj[pl.ds(r0, RB), 0:DH]
        k = proj[pl.ds(r0, RB), DH : 2 * DH]
        hg[pl.ds(r0, RB), 0:DH] = back_norm(q, gain_q, dq[pl.ds(s0, RB), :] * scale).astype(BF16)
        hg[pl.ds(r0, RB), DH : 2 * DH] = back_norm(
            k, gain_k, dk[pl.ds(s0, RB), :] * scale
        ).astype(BF16)
        hg[pl.ds(r0, RB), 2 * DH :] = dv[pl.ds(s0, RB), :].astype(BF16)


def attention_call(img, mv, proj, up, gain):
    vmem = pl.BlockSpec(memory_space=pltpu.VMEM)
    smem = pl.BlockSpec(memory_space=pltpu.SMEM)
    return pl.pallas_call(
        attention_kernel,
        name="attention",
        out_shape=(
            jax.ShapeDtypeStruct((GR, DH), BF16),
            jax.ShapeDtypeStruct((GR, 3 * DH), BF16),
        ),
        in_specs=[smem, smem, vmem, vmem, vmem],
        out_specs=(vmem, vmem),
        scratch_shapes=[
            pltpu.VMEM((GR + TQ, 2 * DH), BF16),
            pltpu.VMEM((GR + TK, 2 * DH), BF16),
            pltpu.VMEM((GR + TK, 2 * DH), BF16),
            pltpu.VMEM((GR + TQ, 2 * DH), BF16),
            pltpu.VMEM((GR, DH), BF16),
            pltpu.VMEM((SLOTS, TQ, TK), BF16),
            pltpu.VMEM((TQ, TK), F32),
            pltpu.VMEM((TQ, TK), F32),
            pltpu.VMEM((TQ, TK), BF16),
            pltpu.VMEM((TQ, TK), BF16),
            pltpu.VMEM((GR + TQ, 2 * DH), F32),
            pltpu.VMEM((GR + TQ, DH), F32),
            pltpu.VMEM((GR + TK, DH), F32),
            pltpu.VMEM((GR + TK, DH), F32),
            pltpu.SMEM((NC,), jnp.int32),
            pltpu.SMEM((NC,), jnp.int32),
            pltpu.SMEM((NC,), jnp.int32),
            pltpu.SMEM((NC,), jnp.int32),
            pltpu.SMEM((SLOTS,), jnp.int32),
            pltpu.SMEM((SLOTS,), jnp.int32),
        ],
        compiler_params=pltpu.CompilerParams(vmem_limit_bytes=VMEM_LIMIT),
    )(img, mv, proj, up, gain)


STEPS = (2, 3, 1, 0)
FC = 4 * SHARD
PART = SHARD // 2


def reduce_kernel(
    rows, hg, grad,
    xs, dw, pair, su, ru, sd, rd,
    xsem, ps, pr, us, ur, ds, dr,
):
    dp = lax.axis_index("dp")
    z, core = dp // 2, dp % 2
    other = {"dp": z * 2 + 1 - core}

    def to_z(step):
        return {"dp": lax.rem(z + step + 8, 8) * 2 + core}

    def chunk(n):
        return lax.rem(z // 2 + STEPS[n], 4)

    def load(n):
        return pltpu.make_async_copy(
            rows.at[:, pl.ds(aligned(chunk(n) * FC, 128), FC)], xs.at[n], xsem.at[n]
        )

    load(0).start()
    load(1).start()
    barrier = pltpu.get_barrier_semaphore()
    for device in (other, to_z(1), to_z(-1)):
        pl.semaphore_signal(barrier, inc=1, device_id=device, device_id_type=MESH)

    def compute(n):
        load(n).wait()
        if n < 2:
            load(n + 2).start()
        m = chunk(n)
        dw[m] = lax.dot_general(xs[n], hg[...], TN, preferred_element_type=F32)

    def pair_copy(n, j):
        m = chunk(n)
        return pltpu.make_async_remote_copy(
            dw.at[m, pl.ds(aligned((2 * j + 1 - core) * SHARD, 16), SHARD), :],
            pair.at[2 * m + j],
            ps.at[n, j], pr.at[n, j], device_id=other, device_id_type=MESH,
        )

    def pair_send(n):
        for j in range(2):
            pair_copy(n, j).start()

    def pair_wait(n):
        for j in range(2):
            pair_copy(n, j).wait_recv()

    def part(dz, b):
        zz = lax.rem(z + dz + 8, 8)
        at = aligned((lax.rem(zz, 2) * 2 + core) * SHARD + b * PART, 16)
        return dw[zz // 2, pl.ds(at, PART), :] + pair[zz, pl.ds(b * PART, PART), :]

    def up_copy(k, b):
        return pltpu.make_async_remote_copy(
            su.at[k, b], ru.at[k, b], us.at[k, b], ur.at[k, b],
            device_id=to_z(1), device_id_type=MESH,
        )

    def down_copy(k, b):
        return pltpu.make_async_remote_copy(
            sd.at[k, b], rd.at[k, b], ds.at[k, b], dr.at[k, b],
            device_id=to_z(-1), device_id_type=MESH,
        )

    def go_up(k):
        for b in range(2):
            value = part(4 - k, b)
            if k:
                up_copy(k - 1, b).wait_recv()
                value = value + ru[k - 1, b].astype(F32)
            su[k, b] = value.astype(BF16)
            up_copy(k, b).start()

    def go_down(k):
        for b in range(2):
            value = part(k - 3, b)
            if k:
                down_copy(k - 1, b).wait_recv()
                value = value + rd[k - 1, b].astype(F32)
            sd[k, b] = value.astype(BF16)
            down_copy(k, b).start()

    compute(0)
    pl.semaphore_wait(barrier, 3)
    pair_send(0)
    compute(1)
    pair_send(1)
    pair_wait(0)
    go_up(0)
    compute(2)
    pair_send(2)
    pair_wait(1)
    go_down(0)
    compute(3)
    pair_send(3)
    pair_wait(2)
    go_up(1)
    go_down(1)
    go_up(2)
    pair_wait(3)
    go_down(2)
    go_up(3)
    for b in range(2):
        total = part(0, b)
        down_copy(2, b).wait_recv()
        total = total + rd[2, b].astype(F32)
        up_copy(3, b).wait_recv()
        grad[b * PART : (b + 1) * PART, :] = total + ru[3, b].astype(F32)
    for n in range(4):
        for j in range(2):
            pair_copy(n, j).wait_send()
    for b in range(2):
        for k in range(4):
            up_copy(k, b).wait_send()
        for k in range(3):
            down_copy(k, b).wait_send()


def reduce_call(rows, hg):
    vmem = pl.BlockSpec(memory_space=pltpu.VMEM)
    hbm = pl.BlockSpec(memory_space=pl.ANY)
    dma = pltpu.SemaphoreType.DMA
    wide = 3 * DH
    return pl.pallas_call(
        reduce_kernel,
        name="grad_reduce",
        out_shape=jax.ShapeDtypeStruct((SHARD, wide), F32),
        in_specs=[hbm, vmem],
        out_specs=vmem,
        scratch_shapes=[
            pltpu.VMEM((4, GR, FC), BF16),
            pltpu.VMEM((4, FC, wide), F32),
            pltpu.VMEM((8, SHARD, wide), F32),
            pltpu.VMEM((4, 2, PART, wide), BF16),
            pltpu.VMEM((4, 2, PART, wide), BF16),
            pltpu.VMEM((3, 2, PART, wide), BF16),
            pltpu.VMEM((3, 2, PART, wide), BF16),
            dma((4,)), dma((4, 2)), dma((4, 2)),
            dma((4, 2)), dma((4, 2)), dma((3, 2)), dma((3, 2)),
        ],
        compiler_params=pltpu.CompilerParams(
            collective_id=1, has_side_effects=True, vmem_limit_bytes=VMEM_LIMIT
        ),
    )(rows, hg)


def body(tokens, modulation, img_size, text_count, move_list, w_qkv, qk_gain, cotangent):
    moves = move_list.transpose(1, 2, 0)
    sizes = img_size.T
    gathered, projected, upstream = gather_call(
        sizes, text_count.T, moves, tokens, modulation, w_qkv, cotangent
    )
    attended, head_grads = attention_call(sizes, moves, projected, upstream, qk_gain)
    return (attended, reduce_call(gathered, head_grads))


def solution(mesh):
    placed = (
        P(("dp", "seq"), None),
        P(None, "dp", None),
        P(),
        P(),
        P(),
        P("dp", "seq"),
        P(None, "seq"),
        P(("dp", "seq"), None),
    )
    return jax.shard_map(
        body,
        mesh=mesh,
        in_specs=placed,
        out_specs=(P("dp", "seq"), P("dp", "seq")),
        check_vma=False,
    )
```

```python
import math

import jax
import jax.numpy as jnp
from jax import lax
from jax.experimental import pallas as pl
from jax.experimental.pallas import tpu as pltpu
from jax.sharding import PartitionSpec as P

EPSILON = 1e-06
MESH = pl.DeviceIdType.MESH
F32 = jnp.float32
BF16 = jnp.bfloat16
D = 2560
DH = 128
RB = 128
NC = 16
NG = 16
GR = NC * RB
CHUNKS = 5
CW = D // CHUNKS
PW = CW // 2
HALF = RB // 2
QUART = HALF // 2
SHARD = D // NG
LAST = (6, 7, 10, 11, 14, 15, 18, 19)
TN = (((0,), (0,)), ((), ()))
NT = (((1,), (1,)), ((), ()))
VMEM_LIMIT = 60 << 20


def aligned(value, step):
    return pl.multiple_of(value, step)


def anchor_of(mv, column, group):
    anchor = group
    for k in range(4):
        anchor = jnp.where(mv[k, 1, column] == group, mv[k, 0, column], anchor)
    return anchor


def gather_kernel(
    img, txt, mv, tok_in, mod_in, w, cot,
    gout, proj_out, up,
    tok, mod, proj, modv, load_sems, proj_sem, *scratch,
):
    load_tok = pltpu.make_async_copy(tok_in, tok, load_sems.at[0])
    load_mod = pltpu.make_async_copy(mod_in, mod, load_sems.at[1])
    load_tok.start()
    load_mod.start()
    st1 = scratch[:CHUNKS]
    st2, gath, wfull, m1s, m1r, m2s, m2r, gs, gr, gf, *scratch = scratch[CHUNKS:]
    wus, wur, wds, wdr, wss, wsr, wl, cs, cr, ls = scratch
    dp = lax.axis_index("dp")
    sq = lax.axis_index("seq")
    z, core = dp // 2, dp % 2
    y, x = sq // 4, sq % 4

    barrier = pltpu.get_barrier_semaphore()

    groups = [lax.rem(dp + k, 16) for k in range(16)]
    columns = [lax.rem(sq + k, 16) for k in range(16)]
    for k in range(1, 16):
        pl.semaphore_signal(
            barrier, inc=1, device_id={"dp": groups[k]}, device_id_type=MESH
        )
        pl.semaphore_signal(
            barrier, inc=1, device_id={"seq": columns[k]}, device_id_type=MESH
        )
    piece_rows = [aligned(d // 2 * 16, 16) for d in groups]
    piece_cols = [aligned(lax.rem(d, 2) * PW, PW) for d in groups]
    ys = [lax.rem(y + k, 4) for k in range(4)]
    xs = [lax.rem(x + k, 4) for k in range(4)]
    bases = [[(ys[j] * 4 + xs[i]) * RB for i in range(4)] for j in range(4)]
    anchors = [anchor_of(mv, sq, d) for d in range(16)]

    first = sq * RB
    slot = jnp.int32(0)
    start = jnp.int32(0)
    end = jnp.int32(0)
    for i in range(8):
        end = end + img[i, dp]
        hit = first >= end
        slot = slot + hit.astype(jnp.int32)
        start = jnp.where(hit, end, start)
    slot = jnp.minimum(slot, 7)
    limit = txt[slot, dp] - (first - start)

    load_tok.wait()
    load_mod.wait()

    @pl.loop(0, RB // 16)
    def _(i):
        r0 = aligned(i * 16, 16)
        rows = tok[pl.ds(r0, 16), :].astype(F32)
        centre = jnp.mean(rows, axis=1, keepdims=True)
        offsets = rows - centre
        variance = jnp.mean(offsets * offsets, axis=1, keepdims=True)
        normed = offsets * lax.rsqrt(variance + EPSILON)
        is_text = lax.broadcasted_iota(jnp.int32, (16, 1), 0) + r0 < limit
        shift = jnp.where(is_text, mod[2, pl.ds(slot, 1), :], mod[0, pl.ds(slot, 1), :])
        scale = jnp.where(is_text, mod[3, pl.ds(slot, 1), :], mod[1, pl.ds(slot, 1), :])
        modv[pl.ds(r0, 16), :] = (normed * (1.0 + scale) + shift).astype(BF16)

    pl.semaphore_wait(barrier, 30)

    def cot_copy(h):
        return pltpu.make_async_remote_copy(
            cot.at[:, pl.ds(aligned(h * DH, DH), DH)],
            up.at[pl.ds(aligned(sq * RB, RB), RB), :],
            cs, cr, device_id={"seq": h}, device_id_type=MESH,
        )

    def send_cot():
        pltpu.make_async_copy(
            cot.at[:, pl.ds(aligned(sq * DH, DH), DH)],
            up.at[pl.ds(aligned(sq * RB, RB), RB), :],
            cr,
        ).start()

        for k in range(1, 16):
            cot_copy(columns[k]).start()

    def send_m1(t):
        for k in range(16):
            piece = modv.at[pl.ds(piece_rows[k], 16), pl.ds(t * CW + piece_cols[k], PW)]
            if k == 0:
                pltpu.make_async_copy(piece, st1[t].at[dp], m1r.at[t]).start()
            else:
                pltpu.make_async_remote_copy(
                    piece, st1[t].at[dp], m1s.at[t], m1r.at[t],
                    device_id={"dp": groups[k]}, device_id_type=MESH,
                ).start()

    def send_m2(t):
        pltpu.make_async_copy(st1[t], st1[t], m1r.at[t]).wait()
        for d in range(16):
            st2[t, d] = st1[t][anchors[d]]
        place = gath.at[
            pl.ds(aligned(sq * RB + piece_rows[0], 16), 16), pl.ds(t * CW + piece_cols[0], PW)
        ]
        pltpu.make_async_copy(st2.at[t, dp], place, m2r.at[t]).start()
        for k in range(1, 16):
            pltpu.make_async_remote_copy(
                st2.at[t, groups[k]], place, m2s.at[t], m2r.at[t],
                device_id={"dp": groups[k]}, device_id_type=MESH,
            ).start()

    def base(h, i, j):
        if h == 0:
            return bases[j % 4][i % 4]
        return bases[i % 4][j % 4]

    def beside(along_x, step):
        if along_x:
            return {"seq": ys[0] * 4 + xs[step % 4]}
        return {"seq": ys[step % 4] * 4 + xs[0]}

    def region(t, h, i, j, part):
        low = base(h, i, j) + h * HALF + (QUART if part == 2 else 0)
        count = HALF if part == 0 else QUART
        return gath.at[pl.ds(aligned(low, QUART), count), pl.ds(t * CW, CW)]

    offsets = (0, -1, 1, 2)

    def event(t, h, e):
        if e < 4:
            along_x = h == 0
            i, j = {0: (0, 0), 1: (0, 0), 2: (-1, 0), 3: (1, 0)}[e]
            gi, gj = {0: (-1, 0), 1: (1, 0), 2: (2, 0), 3: (2, 0)}[e]
            kind = e
        else:
            along_x = h == 1
            k, kind = (e - 4) // 4, (e - 4) % 4
            o = offsets[k]
            i, j = o, {0: 0, 1: 0, 2: -1, 3: 1}[kind]
            gi, gj = o, {0: -1, 1: 1, 2: 2, 3: 2}[kind]
        part = {0: 0, 1: 0, 2: 1, 3: 2}[kind]
        step = 1 if kind in (0, 2) else -1
        return (i, j, gi, gj, part, along_x, step)

    def put(t, h, e):
        i, j, _, _, part, along_x, step = event(t, h, e)
        place = region(t, h, i, j, part)
        pltpu.make_async_remote_copy(
            place, place, gs.at[t], gf.at[t] if e in LAST else gr.at[t, h, e],
            device_id=beside(along_x, step), device_id_type=MESH,
        ).start()

    def got(t, h, e):
        _, _, gi, gj, part, _, _ = event(t, h, e)
        place = region(t, h, gi, gj, part)
        pltpu.make_async_copy(place, place, gr.at[t, h, e]).wait()

    def stage2(t):
        place = gath.at[pl.ds(aligned(sq * RB, RB), RB), pl.ds(t * CW, CW)]
        pltpu.make_async_copy(place, place, m2r.at[t]).wait()
        for e in (0, 1, 4, 5):
            for h in (0, 1):
                put(t, h, e)

    def stage3(t):
        for h in (0, 1):
            got(t, h, 0)
            for e in (2, 8, 9):
                put(t, h, e)
        for h in (0, 1):
            got(t, h, 1)
            for e in (3, 12, 13):
                put(t, h, e)
        for h in (0, 1):
            for kind in (0, 1):
                got(t, h, 4 + kind)
                put(t, h, 6 + kind)

    def stage4(t):
        for h in (0, 1):
            got(t, h, 2)
            got(t, h, 3)
            for e in (16, 17):
                put(t, h, e)
        for k in (1, 2):
            for h in (0, 1):
                for kind in (0, 1):
                    got(t, h, 4 + 4 * k + kind)
                    put(t, h, 6 + 4 * k + kind)

    def stage5(t):
        for h in (0, 1):
            for kind in (0, 1):
                got(t, h, 16 + kind)
                put(t, h, 18 + kind)

    def stage6(t):
        place = gath.at[pl.ds(0, 16 * QUART), pl.ds(t * CW, CW)]
        pltpu.make_async_copy(place, place, gf.at[t]).wait()
        pltpu.make_async_copy(
            gath.at[:, pl.ds(t * CW, CW)], gout.at[:, pl.ds(t * CW, CW)], ls.at[t]
        ).start()

        @pl.loop(0, GR // 256)
        def _(i):
            r0 = aligned(i * 256, 256)
            term = jnp.dot(
                gath[pl.ds(r0, 256), pl.ds(t * CW, CW)],
                wfull[pl.ds(t * CW, CW), :],
                preferred_element_type=F32,
            )
            if t == 0:
                proj[pl.ds(r0, 256), :] = term
            else:
                proj[pl.ds(r0, 256), :] += term
            if t == CHUNKS - 1:
                pltpu.make_async_copy(
                    proj.at[pl.ds(r0, 256), :], proj_out.at[pl.ds(r0, 256), :], proj_sem
                ).start()

    def shard(dz, c):
        return wfull.at[pl.ds(aligned((lax.rem(z + dz + 8, 8) * 2 + c) * SHARD, 16), SHARD), :]

    def to_z(step):
        return {"dp": lax.rem(z + step + 8, 8) * 2 + core}

    def w_put(src, dst, ssem, rsem, device):
        pltpu.make_async_remote_copy(
            src, dst, ssem, rsem, device_id=device, device_id_type=MESH
        ).start()

    def w_got(place, sem):
        pltpu.make_async_copy(place, place, sem).wait()

    other = {"dp": z * 2 + 1 - core}

    def weights(step):
        if step == 0:
            own = shard(0, core)
            pltpu.make_async_copy(w, own, wl).start()
            w_put(w, own, wus.at[0], wur.at[0], to_z(1))
            w_put(w, own, wds.at[0], wdr.at[0], to_z(-1))
            w_put(w, own, wss.at[0], wsr.at[0], other)
            return
        if step <= 4:
            place = shard(-step, core)
            w_got(place, wur.at[step - 1])
            if step < 4:
                w_put(place, place, wus.at[step], wur.at[step], to_z(1))
            w_put(place, place, wss.at[step], wsr.at[step], other)
        if step <= 3:
            place = shard(step, core)
            w_got(place, wdr.at[step - 1])
            if step < 3:
                w_put(place, place, wds.at[step], wdr.at[step], to_z(-1))
            w_put(place, place, wss.at[4 + step], wsr.at[4 + step], other)

    sib_order = (0, -1, -2, -3, -4, 1, 2, 3)

    def weights_end():
        w_got(shard(0, core), wl)
        for k in range(8):
            w_got(shard(sib_order[k], 1 - core), wsr.at[k])

    send_m1(0)
    send_cot()
    stages = ((5, stage5), (4, stage4), (3, stage3), (2, stage2))
    for n in range(CHUNKS + 5):
        for s, run in stages:
            t = n - s + 1
            if 0 <= t < CHUNKS:
                run(t)
        if n < CHUNKS:
            send_m2(n)
        if n == 0:
            send_m1(1)
        if n + 2 < CHUNKS:
            send_m1(n + 2)
        if n <= 4:
            weights(n)
        if n == 5:
            weights_end()
        if 0 <= n - 5 < CHUNKS:
            stage6(n - 5)

    pltpu.make_async_copy(up, up, cr).wait()
    part = up.at[pl.ds(0, 15 * RB), :]
    pltpu.make_async_copy(part, part, cs).wait()
    for t in range(CHUNKS):
        part = st1[t].at[pl.ds(0, 15)]
        pltpu.make_async_copy(part, part, m1s.at[t]).wait()
        pltpu.make_async_copy(part, part, m2s.at[t]).wait()
        part = gath.at[pl.ds(0, 20 * (HALF + QUART)), pl.ds(t * CW, CW)]
        pltpu.make_async_copy(part, part, gs.at[t]).wait()
        pltpu.make_async_copy(
            gath.at[:, pl.ds(t * CW, CW)], gout.at[:, pl.ds(t * CW, CW)], ls.at[t]
        ).wait()
    pltpu.make_async_copy(proj, proj_out, proj_sem).wait()
    own = shard(0, core)
    for k in range(4):
        w_got(own, wus.at[k])
    for k in range(3):
        w_got(own, wds.at[k])
    for k in range(8):
        w_got(own, wss.at[k])


def gather_call(img, txt, mv, tok, mod, w, cot):
    smem = pl.BlockSpec(memory_space=pltpu.SMEM)
    hbm = pl.BlockSpec(memory_space=pl.ANY)
    dma = pltpu.SemaphoreType.DMA
    return pl.pallas_call(
        gather_kernel,
        name="gather_project",
        out_shape=(
            jax.ShapeDtypeStruct((GR, D), BF16),
            jax.ShapeDtypeStruct((GR, 3 * DH), F32),
            jax.ShapeDtypeStruct((GR, DH), BF16),
        ),
        in_specs=[smem, smem, smem, hbm, hbm, hbm, hbm],
        out_specs=(hbm, hbm, hbm),
        scratch_shapes=[
            pltpu.VMEM((RB, D), BF16),
            pltpu.VMEM((4, 8, D), F32),
            pltpu.VMEM((GR, 3 * DH), F32),
            pltpu.VMEM((RB, D), BF16),
            dma((2,)), dma(()),
            *[pltpu.VMEM((16, 16, PW), BF16)] * CHUNKS,
            pltpu.VMEM((CHUNKS, 16, 16, PW), BF16),
            pltpu.VMEM((GR, D), BF16),
            pltpu.VMEM((D, 3 * DH), BF16),
            dma((CHUNKS,)), dma((CHUNKS,)), dma((CHUNKS,)), dma((CHUNKS,)),
            dma((CHUNKS,)), dma((CHUNKS, 2, 20)), dma((CHUNKS,)),
            dma((4,)), dma((4,)), dma((3,)), dma((3,)), dma((8,)), dma((8,)), dma(()),
            dma(()), dma(()), dma((CHUNKS,)),
        ],
        compiler_params=pltpu.CompilerParams(
            collective_id=0, has_side_effects=True, vmem_limit_bytes=VMEM_LIMIT
        ),
    )(img, txt, mv, tok, mod, w, cot)


MASK = 4096.0
TQ = 4 * RB
TK = 4 * RB
NQ = GR // TQ
NK = GR // TK
SLOTS = NQ * NK + 6
PIECES = 4
PIECE = GR // PIECES


def attention_kernel(
    img, mv, proj_in, up_in, gain,
    att_out, hg_out,
    proj, up, att, hg,
    qx, kx, vx, ux, us, es, sa, sb, da, db, oa, dq, dk, dv, place, back, low, high, lq, lk,
    sems, out_sem,
):
    def load(part):
        rows = pl.ds(part * PIECE, PIECE)
        return pltpu.make_async_copy(proj_in.at[rows, :], proj.at[rows, :], sems.at[part])

    load_up = pltpu.make_async_copy(up_in, up, sems.at[PIECES])
    load(0).start()
    load_up.start()
    for part in range(1, PIECES):
        load(part).start()
    group = lax.axis_index("dp")
    scale = 1.0 / math.sqrt(DH)
    segs = []
    for c in range(NC):
        anchor = anchor_of(mv, c, group)
        slot = jnp.int32(0)
        end = jnp.int32(0)
        for i in range(8):
            end = end + img[i, anchor]
            slot = slot + (c * RB >= end).astype(jnp.int32)
        segs.append(anchor * 8 + slot)
    same = [jnp.int32(1)] * NC
    ahead = [jnp.int32(0)] * NC
    for c in range(NC):
        for o in range(c):
            equal = (segs[o] == segs[c]).astype(jnp.int32)
            same[c] = same[c] + equal
            same[o] = same[o] + equal
            ahead[c] = ahead[c] + equal
    keys = [(NC - same[c]) * 256 + segs[c] for c in range(NC)]
    less = [jnp.int32(0)] * NC
    for c in range(NC):
        for o in range(c):
            below = (keys[o] < keys[c]).astype(jnp.int32)
            above = (keys[o] > keys[c]).astype(jnp.int32)
            less[c] = less[c] + below
            less[o] = less[o] + above
    for c in range(NC):
        spot = less[c] + ahead[c]
        place[c] = spot
        back[spot] = c
        low[spot] = less[c]
        high[spot] = less[c] + same[c]

    for i in range(2):
        lq[i] = NQ
        lk[i] = NK

    def list_row(qt, n):
        first = low[qt * (TQ // RB)] // (TK // RB)
        last = (high[qt * (TQ // RB) + TQ // RB - 1] + TK // RB - 1) // (TK // RB)

        def one(kt, n):
            lq[n] = qt
            lk[n] = kt
            return n + 1

        return lax.fori_loop(first, last, one, n)

    count = lax.fori_loop(0, NQ, list_row, jnp.int32(2))
    for i in range(4):
        lq[count + i] = NQ
        lk[count + i] = NK
    steps = (count + 1) // 2

    lanes = lax.broadcasted_iota(jnp.int32, (RB, DH), 1)
    gain_q = gain[0:1, :]
    gain_k = gain[1:2, :]

    def prepare(c):
        r0 = aligned(c * RB, RB)
        spot = place[c]
        s0 = aligned(spot * RB, RB)
        mark = low[spot]
        q = proj[pl.ds(r0, RB), 0:DH]
        k = proj[pl.ds(r0, RB), DH : 2 * DH]
        qi = lax.rsqrt(jnp.mean(q * q, axis=1, keepdims=True) + EPSILON)
        ki = lax.rsqrt(jnp.mean(k * k, axis=1, keepdims=True) + EPSILON)
        qx[pl.ds(s0, RB), 0:DH] = (q * qi * gain_q).astype(BF16)
        kx[pl.ds(s0, RB), 0:DH] = (k * ki * gain_k).astype(BF16)
        vx[pl.ds(s0, RB), 0:DH] = proj[pl.ds(r0, RB), 2 * DH : 3 * DH].astype(BF16)
        hot = lanes == mark
        tail = lanes == NC
        qx[pl.ds(s0, RB), DH:] = jnp.where(hot, MASK, jnp.where(tail, 1.0, 0.0)).astype(BF16)
        kx[pl.ds(s0, RB), DH:] = jnp.where(hot, 1.0, jnp.where(tail, -MASK, 0.0)).astype(BF16)
        vx[pl.ds(s0, RB), DH:] = jnp.full((RB, DH), -1.0, BF16)
        us[pl.ds(s0, RB), :] = up[pl.ds(r0, RB), :]

    load_up.wait()
    for part in range(PIECES):
        load(part).wait()
        for c in range(part * NC // PIECES, (part + 1) * NC // PIECES):
            prepare(c)

    oa[...] = jnp.zeros_like(oa)
    dq[...] = jnp.zeros_like(dq)
    dk[...] = jnp.zeros_like(dk)
    dv[...] = jnp.zeros_like(dv)
    factor = scale * math.log2(math.e)

    def rows_q(i):
        return pl.ds(aligned(lq[i] * TQ, TQ), TQ)

    def rows_k(i):
        return pl.ds(aligned(lk[i] * TK, TK), TK)

    def forward(i, mine, other):
        oa[rows_q(i), :] += jnp.dot(es[i], vx[rows_k(i), :], preferred_element_type=F32)
        es[i + 1] = jnp.exp2(other[...] * factor).astype(BF16)
        mine[...] = lax.dot_general(
            qx[rows_q(i + 2), :], kx[rows_k(i + 2), :], NT, preferred_element_type=F32
        )

    @pl.loop(0, steps)
    def _(j):
        forward(2 * j, sa, sb)
        forward(2 * j + 1, sb, sa)

    @pl.loop(0, NC, unroll=4)
    def _(b):
        s0 = aligned(b * RB, RB)
        inverse = -1.0 / oa[pl.ds(s0, RB), DH:]
        out = (oa[pl.ds(s0, RB), :DH] * inverse).astype(BF16)
        att[pl.ds(aligned(back[b] * RB, RB), RB), :] = out
        scaled = us[pl.ds(s0, RB), :].astype(F32) * inverse
        ux[pl.ds(s0, RB), :DH] = scaled.astype(BF16)
        ux[pl.ds(s0, RB), DH:] = (scaled * out.astype(F32)).astype(BF16)

    att_copy = pltpu.make_async_copy(att, att_out, out_sem.at[0])
    att_copy.start()

    def backward(i, mine, other, ds_mine, ds_other):
        q_rows = rows_q(i)
        k_rows = rows_k(i)
        dv[k_rows, :] += lax.dot_general(
            es[i], ux[q_rows, :DH], TN, preferred_element_type=F32
        )
        ds = ds_other[...]
        dk[k_rows, :] += lax.dot_general(ds, qx[q_rows, :DH], TN, preferred_element_type=F32)
        dq[q_rows, :] += jnp.dot(ds, kx[k_rows, :DH], preferred_element_type=F32)
        ds_mine[...] = (es[i + 1].astype(F32) * other[...]).astype(BF16)
        mine[...] = lax.dot_general(
            ux[rows_q(i + 2), :], vx[rows_k(i + 2), :], NT, preferred_element_type=F32
        )

    @pl.loop(0, steps)
    def _(j):
        backward(2 * j, sa, sb, da, db)
        backward(2 * j + 1, sb, sa, db, da)

    def finish(c):
        r0 = aligned(c * RB, RB)
        s0 = aligned(place[c] * RB, RB)

        def back_norm(values, gains, upstream):
            inverse = lax.rsqrt(jnp.mean(values * values, axis=1, keepdims=True) + EPSILON)
            scaled = upstream * gains
            inner = jnp.mean(scaled * values, axis=1, keepdims=True)
            return inverse * scaled - values * (inverse * inverse * inverse * inner)

        q = proj[pl.ds(r0, RB), 0:DH]
        k = proj[pl.ds(r0, RB), DH : 2 * DH]
        hg[pl.ds(r0, RB), 0:DH] = back_norm(q, gain_q, dq[pl.ds(s0, RB), :] * scale).astype(BF16)
        hg[pl.ds(r0, RB), DH : 2 * DH] = back_norm(
            k, gain_k, dk[pl.ds(s0, RB), :] * scale
        ).astype(BF16)
        hg[pl.ds(r0, RB), 2 * DH :] = dv[pl.ds(s0, RB), :].astype(BF16)

    def store(part):
        rows = pl.ds(part * PIECE, PIECE)
        return pltpu.make_async_copy(hg.at[rows, :], hg_out.at[rows, :], out_sem.at[part + 1])

    for part in range(PIECES):
        for c in range(part * NC // PIECES, (part + 1) * NC // PIECES):
            finish(c)
        store(part).start()
    att_copy.wait()
    for part in range(PIECES):
        store(part).wait()


def attention_call(img, mv, proj, up, gain):
    vmem = pl.BlockSpec(memory_space=pltpu.VMEM)
    hbm = pl.BlockSpec(memory_space=pl.ANY)
    smem = pl.BlockSpec(memory_space=pltpu.SMEM)
    return pl.pallas_call(
        attention_kernel,
        name="attention",
        out_shape=(
            jax.ShapeDtypeStruct((GR, DH), BF16),
            jax.ShapeDtypeStruct((GR, 3 * DH), BF16),
        ),
        in_specs=[smem, smem, hbm, hbm, vmem],
        out_specs=(hbm, hbm),
        scratch_shapes=[
            pltpu.VMEM((GR, 3 * DH), F32),
            pltpu.VMEM((GR, DH), BF16),
            pltpu.VMEM((GR, DH), BF16),
            pltpu.VMEM((GR, 3 * DH), BF16),
            pltpu.VMEM((GR + TQ, 2 * DH), BF16),
            pltpu.VMEM((GR + TK, 2 * DH), BF16),
            pltpu.VMEM((GR + TK, 2 * DH), BF16),
            pltpu.VMEM((GR + TQ, 2 * DH), BF16),
            pltpu.VMEM((GR, DH), BF16),
            pltpu.VMEM((SLOTS, TQ, TK), BF16),
            pltpu.VMEM((TQ, TK), F32),
            pltpu.VMEM((TQ, TK), F32),
            pltpu.VMEM((TQ, TK), BF16),
            pltpu.VMEM((TQ, TK), BF16),
            pltpu.VMEM((GR + TQ, 2 * DH), F32),
            pltpu.VMEM((GR + TQ, DH), F32),
            pltpu.VMEM((GR + TK, DH), F32),
            pltpu.VMEM((GR + TK, DH), F32),
            pltpu.SMEM((NC,), jnp.int32),
            pltpu.SMEM((NC,), jnp.int32),
            pltpu.SMEM((NC,), jnp.int32),
            pltpu.SMEM((NC,), jnp.int32),
            pltpu.SMEM((SLOTS,), jnp.int32),
            pltpu.SMEM((SLOTS,), jnp.int32),
            pltpu.SemaphoreType.DMA((PIECES + 1,)),
            pltpu.SemaphoreType.DMA((PIECES + 1,)),
        ],
        compiler_params=pltpu.CompilerParams(vmem_limit_bytes=VMEM_LIMIT),
    )(img, mv, proj, up, gain)


STEPS = (2, 3, 1, 0)
FC = 4 * SHARD
PART = SHARD // 2
UP = (4, 3)
DOWN = (3, 4)


def reduce_kernel(
    rows, hg_in, grad,
    hg, hg_sem, xs, dw, pair, su, ru, sd, rd,
    xsem, ps, pr, us, ur, ds, dr,
):
    dp = lax.axis_index("dp")
    z, core = dp // 2, dp % 2
    other = {"dp": z * 2 + 1 - core}

    def to_z(step):
        return {"dp": lax.rem(z + step + 8, 8) * 2 + core}

    def chunk(n):
        return lax.rem(z // 2 + STEPS[n], 4)

    def load(n):
        return pltpu.make_async_copy(
            rows.at[:, pl.ds(aligned(chunk(n) * FC, 128), FC)], xs.at[n], xsem.at[n]
        )

    load_hg = pltpu.make_async_copy(hg_in, hg, hg_sem)
    load(0).start()
    load_hg.start()
    barrier = pltpu.get_barrier_semaphore()
    for device in (other, to_z(1), to_z(-1)):
        pl.semaphore_signal(barrier, inc=1, device_id=device, device_id_type=MESH)

    def compute(n):
        load(n).wait()
        if n == 0:
            load(1).start()
            load(2).start()
            load_hg.wait()
        if n == 1:
            load(3).start()
        m = chunk(n)
        dw[m] = lax.dot_general(xs[n], hg[...], TN, preferred_element_type=F32)

    def pair_copy(n, j):
        m = chunk(n)
        return pltpu.make_async_remote_copy(
            dw.at[m, pl.ds(aligned((2 * j + 1 - core) * SHARD, 16), SHARD), :],
            pair.at[2 * m + j],
            ps.at[n, j], pr.at[n, j], device_id=other, device_id_type=MESH,
        )

    def pair_send(n):
        for j in range(2):
            pair_copy(n, j).start()

    def pair_wait(n):
        for j in range(2):
            pair_copy(n, j).wait_recv()

    def part(dz, b):
        zz = lax.rem(z + dz + 8, 8)
        at = aligned((lax.rem(zz, 2) * 2 + core) * SHARD + b * PART, 16)
        return dw[zz // 2, pl.ds(at, PART), :] + pair[zz, pl.ds(b * PART, PART), :]

    def up_copy(k, b):
        return pltpu.make_async_remote_copy(
            su.at[k, b], ru.at[k, b], us.at[k, b], ur.at[k, b],
            device_id=to_z(1), device_id_type=MESH,
        )

    def down_copy(k, b):
        return pltpu.make_async_remote_copy(
            sd.at[k, b], rd.at[k, b], ds.at[k, b], dr.at[k, b],
            device_id=to_z(-1), device_id_type=MESH,
        )

    def go_up(k, b):
        value = part(UP[b] - k, b)
        if k:
            up_copy(k - 1, b).wait_recv()
            value = value + ru[k - 1, b].astype(F32)
        su[k, b] = value.astype(BF16)
        up_copy(k, b).start()

    def go_down(k, b):
        value = part(k - DOWN[b], b)
        if k:
            down_copy(k - 1, b).wait_recv()
            value = value + rd[k - 1, b].astype(F32)
        sd[k, b] = value.astype(BF16)
        down_copy(k, b).start()

    compute(0)
    pl.semaphore_wait(barrier, 3)
    pair_send(0)
    compute(1)
    pair_send(1)
    pair_wait(0)
    go_up(0, 0)
    go_down(0, 1)
    compute(2)
    pair_send(2)
    pair_wait(1)
    go_down(0, 0)
    go_down(1, 1)
    compute(3)
    pair_send(3)
    pair_wait(2)
    go_up(0, 1)
    go_up(1, 0)
    go_down(1, 0)
    go_down(2, 1)
    go_up(1, 1)
    go_up(2, 0)
    pair_wait(3)
    go_down(2, 0)
    go_down(3, 1)
    go_up(2, 1)
    go_up(3, 0)
    for b in range(2):
        total = part(0, b)
        down_copy(DOWN[b] - 1, b).wait_recv()
        total = total + rd[DOWN[b] - 1, b].astype(F32)
        up_copy(UP[b] - 1, b).wait_recv()
        grad[b * PART : (b + 1) * PART, :] = total + ru[UP[b] - 1, b].astype(F32)
    for n in range(4):
        for j in range(2):
            pair_copy(n, j).wait_send()
    for b in range(2):
        for k in range(UP[b]):
            up_copy(k, b).wait_send()
        for k in range(DOWN[b]):
            down_copy(k, b).wait_send()


def reduce_call(rows, hg):
    vmem = pl.BlockSpec(memory_space=pltpu.VMEM)
    hbm = pl.BlockSpec(memory_space=pl.ANY)
    dma = pltpu.SemaphoreType.DMA
    wide = 3 * DH
    return pl.pallas_call(
        reduce_kernel,
        name="grad_reduce",
        out_shape=jax.ShapeDtypeStruct((SHARD, wide), F32),
        in_specs=[hbm, hbm],
        out_specs=vmem,
        scratch_shapes=[
            pltpu.VMEM((GR, wide), BF16),
            dma(()),
            pltpu.VMEM((4, GR, FC), BF16),
            pltpu.VMEM((4, FC, wide), F32),
            pltpu.VMEM((8, SHARD, wide), F32),
            pltpu.VMEM((4, 2, PART, wide), BF16),
            pltpu.VMEM((4, 2, PART, wide), BF16),
            pltpu.VMEM((4, 2, PART, wide), BF16),
            pltpu.VMEM((4, 2, PART, wide), BF16),
            dma((4,)), dma((4, 2)), dma((4, 2)),
            dma((4, 2)), dma((4, 2)), dma((4, 2)), dma((4, 2)),
        ],
        compiler_params=pltpu.CompilerParams(
            collective_id=1, has_side_effects=True, vmem_limit_bytes=VMEM_LIMIT
        ),
    )(rows, hg)


def body(tokens, modulation, img_size, text_count, move_list, w_qkv, qk_gain, cotangent):
    moves = move_list.transpose(1, 2, 0)
    sizes = img_size.T
    gathered, projected, upstream = gather_call(
        sizes, text_count.T, moves, tokens, modulation, w_qkv, cotangent
    )
    attended, head_grads = attention_call(sizes, moves, projected, upstream, qk_gain)
    return (attended, reduce_call(gathered, head_grads))


def solution(mesh):
    placed = (
        P(("dp", "seq"), None),
        P(None, "dp", None),
        P(),
        P(),
        P(),
        P("dp", "seq"),
        P(None, "seq"),
        P(("dp", "seq"), None),
    )
    return jax.shard_map(
        body,
        mesh=mesh,
        in_specs=placed,
        out_specs=(P("dp", "seq"), P("dp", "seq")),
        check_vma=False,
    )
```

```python
import math

import jax
import jax.numpy as jnp
from jax import lax
from jax.experimental import pallas as pl
from jax.experimental.pallas import tpu as pltpu
from jax.sharding import PartitionSpec as P

EPSILON = 1e-06
MESH = pl.DeviceIdType.MESH
F32 = jnp.float32
BF16 = jnp.bfloat16
D = 2560
DH = 128
RB = 128
NC = 16
NG = 16
GR = NC * RB
CHUNKS = 5
CW = D // CHUNKS
PW = CW // 2
HALF = RB // 2
QUART = HALF // 2
SHARD = D // NG
LAST = (6, 7, 10, 11, 14, 15, 18, 19)
TN = (((0,), (0,)), ((), ()))
NT = (((1,), (1,)), ((), ()))
VMEM_LIMIT = 60 << 20


def aligned(value, step):
    return pl.multiple_of(value, step)


def anchor_of(mv, column, group):
    anchor = group
    for k in range(4):
        anchor = jnp.where(mv[k, 1, column] == group, mv[k, 0, column], anchor)
    return anchor


def gather_kernel(
    img, txt, mv, tok_in, mod_in, w, cot,
    gout, proj_out, up,
    tok, mod, proj, modv, load_sems, proj_sem, *scratch,
):
    load_tok = pltpu.make_async_copy(tok_in, tok, load_sems.at[0])
    load_mod = pltpu.make_async_copy(mod_in, mod, load_sems.at[1])
    load_tok.start()
    load_mod.start()
    st1 = scratch[:CHUNKS]
    st2, gath, wfull, m1s, m1r, m2s, m2r, gs, gr, gf, *scratch = scratch[CHUNKS:]
    wus, wur, wds, wdr, wss, wsr, wl, cs, cr, ls = scratch
    dp = lax.axis_index("dp")
    sq = lax.axis_index("seq")
    z, core = dp // 2, dp % 2
    y, x = sq // 4, sq % 4

    barrier = pltpu.get_barrier_semaphore()

    groups = [lax.rem(dp + k, 16) for k in range(16)]
    columns = [lax.rem(sq + k, 16) for k in range(16)]
    for k in range(1, 16):
        pl.semaphore_signal(
            barrier, inc=1, device_id={"dp": groups[k]}, device_id_type=MESH
        )
        pl.semaphore_signal(
            barrier, inc=1, device_id={"seq": columns[k]}, device_id_type=MESH
        )
    piece_rows = [aligned(d // 2 * 16, 16) for d in groups]
    piece_cols = [aligned(lax.rem(d, 2) * PW, PW) for d in groups]
    ys = [lax.rem(y + k, 4) for k in range(4)]
    xs = [lax.rem(x + k, 4) for k in range(4)]
    bases = [[(ys[j] * 4 + xs[i]) * RB for i in range(4)] for j in range(4)]
    anchors = [anchor_of(mv, sq, d) for d in range(16)]

    first = sq * RB
    slot = jnp.int32(0)
    start = jnp.int32(0)
    end = jnp.int32(0)
    for i in range(8):
        end = end + img[i, dp]
        hit = first >= end
        slot = slot + hit.astype(jnp.int32)
        start = jnp.where(hit, end, start)
    slot = jnp.minimum(slot, 7)
    limit = txt[slot, dp] - (first - start)

    load_tok.wait()
    load_mod.wait()

    @pl.loop(0, RB // 16)
    def _(i):
        r0 = aligned(i * 16, 16)
        rows = tok[pl.ds(r0, 16), :].astype(F32)
        centre = jnp.mean(rows, axis=1, keepdims=True)
        offsets = rows - centre
        variance = jnp.mean(offsets * offsets, axis=1, keepdims=True)
        normed = offsets * lax.rsqrt(variance + EPSILON)
        is_text = lax.broadcasted_iota(jnp.int32, (16, 1), 0) + r0 < limit
        shift = jnp.where(is_text, mod[2, pl.ds(slot, 1), :], mod[0, pl.ds(slot, 1), :])
        scale = jnp.where(is_text, mod[3, pl.ds(slot, 1), :], mod[1, pl.ds(slot, 1), :])
        modv[pl.ds(r0, 16), :] = (normed * (1.0 + scale) + shift).astype(BF16)

    pl.semaphore_wait(barrier, 30)

    def cot_copy(h):
        return pltpu.make_async_remote_copy(
            cot.at[:, pl.ds(aligned(h * DH, DH), DH)],
            up.at[pl.ds(aligned(sq * RB, RB), RB), :],
            cs, cr, device_id={"seq": h}, device_id_type=MESH,
        )

    def send_cot():
        pltpu.make_async_copy(
            cot.at[:, pl.ds(aligned(sq * DH, DH), DH)],
            up.at[pl.ds(aligned(sq * RB, RB), RB), :],
            cr,
        ).start()

        for k in range(1, 16):
            cot_copy(columns[k]).start()

    def send_m1(t):
        for k in range(16):
            piece = modv.at[pl.ds(piece_rows[k], 16), pl.ds(t * CW + piece_cols[k], PW)]
            if k == 0:
                pltpu.make_async_copy(piece, st1[t].at[dp], m1r.at[t]).start()
            else:
                pltpu.make_async_remote_copy(
                    piece, st1[t].at[dp], m1s.at[t], m1r.at[t],
                    device_id={"dp": groups[k]}, device_id_type=MESH,
                ).start()

    def send_m2(t):
        pltpu.make_async_copy(st1[t], st1[t], m1r.at[t]).wait()
        for d in range(16):
            st2[t, d] = st1[t][anchors[d]]
        place = gath.at[
            pl.ds(aligned(sq * RB + piece_rows[0], 16), 16), pl.ds(t * CW + piece_cols[0], PW)
        ]
        pltpu.make_async_copy(st2.at[t, dp], place, m2r.at[t]).start()
        for k in range(1, 16):
            pltpu.make_async_remote_copy(
                st2.at[t, groups[k]], place, m2s.at[t], m2r.at[t],
                device_id={"dp": groups[k]}, device_id_type=MESH,
            ).start()

    def base(h, i, j):
        if h == 0:
            return bases[j % 4][i % 4]
        return bases[i % 4][j % 4]

    def beside(along_x, step):
        if along_x:
            return {"seq": ys[0] * 4 + xs[step % 4]}
        return {"seq": ys[step % 4] * 4 + xs[0]}

    def region(t, h, i, j, part):
        low = base(h, i, j) + h * HALF + (QUART if part == 2 else 0)
        count = HALF if part == 0 else QUART
        return gath.at[pl.ds(aligned(low, QUART), count), pl.ds(t * CW, CW)]

    offsets = (0, -1, 1, 2)

    def event(t, h, e):
        if e < 4:
            along_x = h == 0
            i, j = {0: (0, 0), 1: (0, 0), 2: (-1, 0), 3: (1, 0)}[e]
            gi, gj = {0: (-1, 0), 1: (1, 0), 2: (2, 0), 3: (2, 0)}[e]
            kind = e
        else:
            along_x = h == 1
            k, kind = (e - 4) // 4, (e - 4) % 4
            o = offsets[k]
            i, j = o, {0: 0, 1: 0, 2: -1, 3: 1}[kind]
            gi, gj = o, {0: -1, 1: 1, 2: 2, 3: 2}[kind]
        part = {0: 0, 1: 0, 2: 1, 3: 2}[kind]
        step = 1 if kind in (0, 2) else -1
        return (i, j, gi, gj, part, along_x, step)

    def put(t, h, e):
        i, j, _, _, part, along_x, step = event(t, h, e)
        place = region(t, h, i, j, part)
        pltpu.make_async_remote_copy(
            place, place, gs.at[t], gf.at[t] if e in LAST else gr.at[t, h, e],
            device_id=beside(along_x, step), device_id_type=MESH,
        ).start()

    def got(t, h, e):
        _, _, gi, gj, part, _, _ = event(t, h, e)
        place = region(t, h, gi, gj, part)
        pltpu.make_async_copy(place, place, gr.at[t, h, e]).wait()

    def stage2(t):
        place = gath.at[pl.ds(aligned(sq * RB, RB), RB), pl.ds(t * CW, CW)]
        pltpu.make_async_copy(place, place, m2r.at[t]).wait()
        for e in (0, 1, 4, 5):
            for h in (0, 1):
                put(t, h, e)

    def stage3(t):
        for h in (0, 1):
            got(t, h, 0)
            for e in (2, 8, 9):
                put(t, h, e)
        for h in (0, 1):
            got(t, h, 1)
            for e in (3, 12, 13):
                put(t, h, e)
        for h in (0, 1):
            for kind in (0, 1):
                got(t, h, 4 + kind)
                put(t, h, 6 + kind)

    def stage4(t):
        for h in (0, 1):
            got(t, h, 2)
            got(t, h, 3)
            for e in (16, 17):
                put(t, h, e)
        for k in (1, 2):
            for h in (0, 1):
                for kind in (0, 1):
                    got(t, h, 4 + 4 * k + kind)
                    put(t, h, 6 + 4 * k + kind)

    def stage5(t):
        for h in (0, 1):
            for kind in (0, 1):
                got(t, h, 16 + kind)
                put(t, h, 18 + kind)

    def stage6(t):
        place = gath.at[pl.ds(0, 16 * QUART), pl.ds(t * CW, CW)]
        pltpu.make_async_copy(place, place, gf.at[t]).wait()
        pltpu.make_async_copy(
            gath.at[:, pl.ds(t * CW, CW)], gout.at[:, pl.ds(t * CW, CW)], ls.at[t]
        ).start()

        @pl.loop(0, GR // 256)
        def _(i):
            r0 = aligned(i * 256, 256)
            term = jnp.dot(
                gath[pl.ds(r0, 256), pl.ds(t * CW, CW)],
                wfull[pl.ds(t * CW, CW), :],
                preferred_element_type=F32,
            )
            if t == 0:
                proj[pl.ds(r0, 256), :] = term
            else:
                proj[pl.ds(r0, 256), :] += term
            if t == CHUNKS - 1:
                pltpu.make_async_copy(
                    proj.at[pl.ds(r0, 256), :], proj_out.at[pl.ds(r0, 256), :], proj_sem
                ).start()

    def shard(dz, c):
        return wfull.at[pl.ds(aligned((lax.rem(z + dz + 8, 8) * 2 + c) * SHARD, 16), SHARD), :]

    def to_z(step):
        return {"dp": lax.rem(z + step + 8, 8) * 2 + core}

    def w_put(src, dst, ssem, rsem, device):
        pltpu.make_async_remote_copy(
            src, dst, ssem, rsem, device_id=device, device_id_type=MESH
        ).start()

    def w_got(place, sem):
        pltpu.make_async_copy(place, place, sem).wait()

    other = {"dp": z * 2 + 1 - core}

    def weights(step):
        if step == 0:
            own = shard(0, core)
            pltpu.make_async_copy(w, own, wl).start()
            w_put(w, own, wus.at[0], wur.at[0], to_z(1))
            w_put(w, own, wds.at[0], wdr.at[0], to_z(-1))
            w_put(w, own, wss.at[0], wsr.at[0], other)
            return
        if step <= 4:
            place = shard(-step, core)
            w_got(place, wur.at[step - 1])
            if step < 4:
                w_put(place, place, wus.at[step], wur.at[step], to_z(1))
            w_put(place, place, wss.at[step], wsr.at[step], other)
        if step <= 3:
            place = shard(step, core)
            w_got(place, wdr.at[step - 1])
            if step < 3:
                w_put(place, place, wds.at[step], wdr.at[step], to_z(-1))
            w_put(place, place, wss.at[4 + step], wsr.at[4 + step], other)

    sib_order = (0, -1, -2, -3, -4, 1, 2, 3)

    def weights_end():
        w_got(shard(0, core), wl)
        for k in range(8):
            w_got(shard(sib_order[k], 1 - core), wsr.at[k])

    send_m1(0)
    send_cot()
    stages = ((5, stage5), (4, stage4), (3, stage3), (2, stage2))
    for n in range(CHUNKS + 5):
        for s, run in stages:
            t = n - s + 1
            if 0 <= t < CHUNKS:
                run(t)
        if n < CHUNKS:
            send_m2(n)
        if n + 1 < CHUNKS:
            send_m1(n + 1)
        if n <= 4:
            weights(n)
        if n == 5:
            weights_end()
        if 0 <= n - 5 < CHUNKS:
            stage6(n - 5)

    pltpu.make_async_copy(up, up, cr).wait()
    part = up.at[pl.ds(0, 15 * RB), :]
    pltpu.make_async_copy(part, part, cs).wait()
    for t in range(CHUNKS):
        part = st1[t].at[pl.ds(0, 15)]
        pltpu.make_async_copy(part, part, m1s.at[t]).wait()
        pltpu.make_async_copy(part, part, m2s.at[t]).wait()
        part = gath.at[pl.ds(0, 20 * (HALF + QUART)), pl.ds(t * CW, CW)]
        pltpu.make_async_copy(part, part, gs.at[t]).wait()
        pltpu.make_async_copy(
            gath.at[:, pl.ds(t * CW, CW)], gout.at[:, pl.ds(t * CW, CW)], ls.at[t]
        ).wait()
    pltpu.make_async_copy(proj, proj_out, proj_sem).wait()
    own = shard(0, core)
    for k in range(4):
        w_got(own, wus.at[k])
    for k in range(3):
        w_got(own, wds.at[k])
    for k in range(8):
        w_got(own, wss.at[k])


def gather_call(img, txt, mv, tok, mod, w, cot):
    smem = pl.BlockSpec(memory_space=pltpu.SMEM)
    hbm = pl.BlockSpec(memory_space=pl.ANY)
    dma = pltpu.SemaphoreType.DMA
    return pl.pallas_call(
        gather_kernel,
        name="gather_project",
        out_shape=(
            jax.ShapeDtypeStruct((GR, D), BF16),
            jax.ShapeDtypeStruct((GR, 3 * DH), F32),
            jax.ShapeDtypeStruct((GR, DH), BF16),
        ),
        in_specs=[smem, smem, smem, hbm, hbm, hbm, hbm],
        out_specs=(hbm, hbm, hbm),
        scratch_shapes=[
            pltpu.VMEM((RB, D), BF16),
            pltpu.VMEM((4, 8, D), F32),
            pltpu.VMEM((GR, 3 * DH), F32),
            pltpu.VMEM((RB, D), BF16),
            dma((2,)), dma(()),
            *[pltpu.VMEM((16, 16, PW), BF16)] * CHUNKS,
            pltpu.VMEM((CHUNKS, 16, 16, PW), BF16),
            pltpu.VMEM((GR, D), BF16),
            pltpu.VMEM((D, 3 * DH), BF16),
            dma((CHUNKS,)), dma((CHUNKS,)), dma((CHUNKS,)), dma((CHUNKS,)),
            dma((CHUNKS,)), dma((CHUNKS, 2, 20)), dma((CHUNKS,)),
            dma((4,)), dma((4,)), dma((3,)), dma((3,)), dma((8,)), dma((8,)), dma(()),
            dma(()), dma(()), dma((CHUNKS,)),
        ],
        compiler_params=pltpu.CompilerParams(
            collective_id=0, has_side_effects=True, vmem_limit_bytes=VMEM_LIMIT
        ),
    )(img, txt, mv, tok, mod, w, cot)


MASK = 4096.0
TQ = 4 * RB
TK = 4 * RB
NQ = GR // TQ
NK = GR // TK
SLOTS = NQ * NK + 6
PIECES = 4
PIECE = GR // PIECES


def attention_kernel(
    img, mv, proj_in, up_in, gain,
    att_out, hg_out,
    proj, up, att, hg,
    qx, kx, vx, ux, us, es, sa, sb, da, db, oa, dq, dk, dv, place, back, low, high, lq, lk,
    sems, out_sem,
):
    def load(part):
        rows = pl.ds(part * PIECE, PIECE)
        return pltpu.make_async_copy(proj_in.at[rows, :], proj.at[rows, :], sems.at[part])

    load_up = pltpu.make_async_copy(up_in, up, sems.at[PIECES])
    load(0).start()
    load_up.start()
    for part in range(1, PIECES):
        load(part).start()
    group = lax.axis_index("dp")
    scale = 1.0 / math.sqrt(DH)
    segs = []
    for c in range(NC):
        anchor = anchor_of(mv, c, group)
        slot = jnp.int32(0)
        end = jnp.int32(0)
        for i in range(8):
            end = end + img[i, anchor]
            slot = slot + (c * RB >= end).astype(jnp.int32)
        segs.append(anchor * 8 + slot)
    same = [jnp.int32(1)] * NC
    ahead = [jnp.int32(0)] * NC
    for c in range(NC):
        for o in range(c):
            equal = (segs[o] == segs[c]).astype(jnp.int32)
            same[c] = same[c] + equal
            same[o] = same[o] + equal
            ahead[c] = ahead[c] + equal
    keys = [(NC - same[c]) * 256 + segs[c] for c in range(NC)]
    less = [jnp.int32(0)] * NC
    for c in range(NC):
        for o in range(c):
            below = (keys[o] < keys[c]).astype(jnp.int32)
            above = (keys[o] > keys[c]).astype(jnp.int32)
            less[c] = less[c] + below
            less[o] = less[o] + above
    for c in range(NC):
        spot = less[c] + ahead[c]
        place[c] = spot
        back[spot] = c
        low[spot] = less[c]
        high[spot] = less[c] + same[c]

    for i in range(2):
        lq[i] = NQ
        lk[i] = NK

    def list_row(qt, n):
        first = low[qt * (TQ // RB)] // (TK // RB)
        last = (high[qt * (TQ // RB) + TQ // RB - 1] + TK // RB - 1) // (TK // RB)

        def one(kt, n):
            lq[n] = qt
            lk[n] = kt
            return n + 1

        return lax.fori_loop(first, last, one, n)

    count = lax.fori_loop(0, NQ, list_row, jnp.int32(2))
    for i in range(4):
        lq[count + i] = NQ
        lk[count + i] = NK
    steps = (count + 1) // 2

    lanes = lax.broadcasted_iota(jnp.int32, (RB, DH), 1)
    gain_q = gain[0:1, :]
    gain_k = gain[1:2, :]

    def prepare(c):
        r0 = aligned(c * RB, RB)
        spot = place[c]
        s0 = aligned(spot * RB, RB)
        mark = low[spot]
        q = proj[pl.ds(r0, RB), 0:DH]
        k = proj[pl.ds(r0, RB), DH : 2 * DH]
        qi = lax.rsqrt(jnp.mean(q * q, axis=1, keepdims=True) + EPSILON)
        ki = lax.rsqrt(jnp.mean(k * k, axis=1, keepdims=True) + EPSILON)
        qx[pl.ds(s0, RB), 0:DH] = (q * qi * gain_q).astype(BF16)
        kx[pl.ds(s0, RB), 0:DH] = (k * ki * gain_k).astype(BF16)
        vx[pl.ds(s0, RB), 0:DH] = proj[pl.ds(r0, RB), 2 * DH : 3 * DH].astype(BF16)
        hot = lanes == mark
        tail = lanes == NC
        qx[pl.ds(s0, RB), DH:] = jnp.where(hot, MASK, jnp.where(tail, 1.0, 0.0)).astype(BF16)
        kx[pl.ds(s0, RB), DH:] = jnp.where(hot, 1.0, jnp.where(tail, -MASK, 0.0)).astype(BF16)
        vx[pl.ds(s0, RB), DH:] = jnp.full((RB, DH), -1.0, BF16)
        us[pl.ds(s0, RB), :] = up[pl.ds(r0, RB), :]

    load_up.wait()
    for part in range(PIECES):
        load(part).wait()
        for c in range(part * NC // PIECES, (part + 1) * NC // PIECES):
            prepare(c)

    oa[...] = jnp.zeros_like(oa)
    dq[...] = jnp.zeros_like(dq)
    dk[...] = jnp.zeros_like(dk)
    dv[...] = jnp.zeros_like(dv)
    factor = scale * math.log2(math.e)

    def rows_q(i):
        return pl.ds(aligned(lq[i] * TQ, TQ), TQ)

    def rows_k(i):
        return pl.ds(aligned(lk[i] * TK, TK), TK)

    def forward(i, mine, other):
        oa[rows_q(i), :] += jnp.dot(es[i], vx[rows_k(i), :], preferred_element_type=F32)
        es[i + 1] = jnp.exp2(other[...] * factor).astype(BF16)
        mine[...] = lax.dot_general(
            qx[rows_q(i + 2), :], kx[rows_k(i + 2), :], NT, preferred_element_type=F32
        )

    @pl.loop(0, steps)
    def _(j):
        forward(2 * j, sa, sb)
        forward(2 * j + 1, sb, sa)

    @pl.loop(0, NC, unroll=4)
    def _(b):
        s0 = aligned(b * RB, RB)
        inverse = -1.0 / oa[pl.ds(s0, RB), DH:]
        out = (oa[pl.ds(s0, RB), :DH] * inverse).astype(BF16)
        att[pl.ds(aligned(back[b] * RB, RB), RB), :] = out
        scaled = us[pl.ds(s0, RB), :].astype(F32) * inverse
        ux[pl.ds(s0, RB), :DH] = scaled.astype(BF16)
        ux[pl.ds(s0, RB), DH:] = (scaled * out.astype(F32)).astype(BF16)

    att_copy = pltpu.make_async_copy(att, att_out, out_sem.at[0])
    att_copy.start()

    def backward(i, mine, other, ds_mine, ds_other):
        q_rows = rows_q(i)
        k_rows = rows_k(i)
        dv[k_rows, :] += lax.dot_general(
            es[i], ux[q_rows, :DH], TN, preferred_element_type=F32
        )
        ds = ds_other[...]
        dk[k_rows, :] += lax.dot_general(ds, qx[q_rows, :DH], TN, preferred_element_type=F32)
        dq[q_rows, :] += jnp.dot(ds, kx[k_rows, :DH], preferred_element_type=F32)
        ds_mine[...] = (es[i + 1].astype(F32) * other[...]).astype(BF16)
        mine[...] = lax.dot_general(
            ux[rows_q(i + 2), :], vx[rows_k(i + 2), :], NT, preferred_element_type=F32
        )

    @pl.loop(0, steps)
    def _(j):
        backward(2 * j, sa, sb, da, db)
        backward(2 * j + 1, sb, sa, db, da)

    def finish(c):
        r0 = aligned(c * RB, RB)
        s0 = aligned(place[c] * RB, RB)

        def back_norm(values, gains, upstream):
            inverse = lax.rsqrt(jnp.mean(values * values, axis=1, keepdims=True) + EPSILON)
            scaled = upstream * gains
            inner = jnp.mean(scaled * values, axis=1, keepdims=True)
            return inverse * scaled - values * (inverse * inverse * inverse * inner)

        q = proj[pl.ds(r0, RB), 0:DH]
        k = proj[pl.ds(r0, RB), DH : 2 * DH]
        hg[pl.ds(r0, RB), 0:DH] = back_norm(q, gain_q, dq[pl.ds(s0, RB), :] * scale).astype(BF16)
        hg[pl.ds(r0, RB), DH : 2 * DH] = back_norm(
            k, gain_k, dk[pl.ds(s0, RB), :] * scale
        ).astype(BF16)
        hg[pl.ds(r0, RB), 2 * DH :] = dv[pl.ds(s0, RB), :].astype(BF16)

    def store(part):
        rows = pl.ds(part * PIECE, PIECE)
        return pltpu.make_async_copy(hg.at[rows, :], hg_out.at[rows, :], out_sem.at[part + 1])

    for part in range(PIECES):
        for c in range(part * NC // PIECES, (part + 1) * NC // PIECES):
            finish(c)
        store(part).start()
    att_copy.wait()
    for part in range(PIECES):
        store(part).wait()


def attention_call(img, mv, proj, up, gain):
    vmem = pl.BlockSpec(memory_space=pltpu.VMEM)
    hbm = pl.BlockSpec(memory_space=pl.ANY)
    smem = pl.BlockSpec(memory_space=pltpu.SMEM)
    return pl.pallas_call(
        attention_kernel,
        name="attention",
        out_shape=(
            jax.ShapeDtypeStruct((GR, DH), BF16),
            jax.ShapeDtypeStruct((GR, 3 * DH), BF16),
        ),
        in_specs=[smem, smem, hbm, hbm, vmem],
        out_specs=(hbm, hbm),
        scratch_shapes=[
            pltpu.VMEM((GR, 3 * DH), F32),
            pltpu.VMEM((GR, DH), BF16),
            pltpu.VMEM((GR, DH), BF16),
            pltpu.VMEM((GR, 3 * DH), BF16),
            pltpu.VMEM((GR + TQ, 2 * DH), BF16),
            pltpu.VMEM((GR + TK, 2 * DH), BF16),
            pltpu.VMEM((GR + TK, 2 * DH), BF16),
            pltpu.VMEM((GR + TQ, 2 * DH), BF16),
            pltpu.VMEM((GR, DH), BF16),
            pltpu.VMEM((SLOTS, TQ, TK), BF16),
            pltpu.VMEM((TQ, TK), F32),
            pltpu.VMEM((TQ, TK), F32),
            pltpu.VMEM((TQ, TK), BF16),
            pltpu.VMEM((TQ, TK), BF16),
            pltpu.VMEM((GR + TQ, 2 * DH), F32),
            pltpu.VMEM((GR + TQ, DH), F32),
            pltpu.VMEM((GR + TK, DH), F32),
            pltpu.VMEM((GR + TK, DH), F32),
            pltpu.SMEM((NC,), jnp.int32),
            pltpu.SMEM((NC,), jnp.int32),
            pltpu.SMEM((NC,), jnp.int32),
            pltpu.SMEM((NC,), jnp.int32),
            pltpu.SMEM((SLOTS,), jnp.int32),
            pltpu.SMEM((SLOTS,), jnp.int32),
            pltpu.SemaphoreType.DMA((PIECES + 1,)),
            pltpu.SemaphoreType.DMA((PIECES + 1,)),
        ],
        compiler_params=pltpu.CompilerParams(vmem_limit_bytes=VMEM_LIMIT),
    )(img, mv, proj, up, gain)


STEPS = (2, 3, 1, 0)
FC = 4 * SHARD
PART = SHARD // 2
UP = (4, 3)
DOWN = (3, 4)


def reduce_kernel(
    rows, hg_in, grad,
    hg, hg_sem, xs, dw, pair, su, ru, sd, rd,
    xsem, ps, pr, us, ur, ds, dr,
):
    dp = lax.axis_index("dp")
    z, core = dp // 2, dp % 2
    other = {"dp": z * 2 + 1 - core}

    def to_z(step):
        return {"dp": lax.rem(z + step + 8, 8) * 2 + core}

    def chunk(n):
        return lax.rem(z // 2 + STEPS[n], 4)

    def load(n):
        return pltpu.make_async_copy(
            rows.at[:, pl.ds(aligned(chunk(n) * FC, 128), FC)], xs.at[n], xsem.at[n]
        )

    load_hg = pltpu.make_async_copy(hg_in, hg, hg_sem)
    load(0).start()
    load_hg.start()
    barrier = pltpu.get_barrier_semaphore()
    for device in (other, to_z(1), to_z(-1)):
        pl.semaphore_signal(barrier, inc=1, device_id=device, device_id_type=MESH)

    def compute(n):
        load(n).wait()
        if n == 0:
            load(1).start()
            load(2).start()
            load_hg.wait()
        if n == 1:
            load(3).start()
        m = chunk(n)
        dw[m] = lax.dot_general(xs[n], hg[...], TN, preferred_element_type=F32)

    def pair_copy(n, j):
        m = chunk(n)
        return pltpu.make_async_remote_copy(
            dw.at[m, pl.ds(aligned((2 * j + 1 - core) * SHARD, 16), SHARD), :],
            pair.at[2 * m + j],
            ps.at[n, j], pr.at[n, j], device_id=other, device_id_type=MESH,
        )

    def pair_send(n):
        for j in range(2):
            pair_copy(n, j).start()

    def pair_wait(n):
        for j in range(2):
            pair_copy(n, j).wait_recv()

    def part(dz, b):
        zz = lax.rem(z + dz + 8, 8)
        at = aligned((lax.rem(zz, 2) * 2 + core) * SHARD + b * PART, 16)
        return dw[zz // 2, pl.ds(at, PART), :] + pair[zz, pl.ds(b * PART, PART), :]

    def up_copy(k, b):
        return pltpu.make_async_remote_copy(
            su.at[k, b], ru.at[k, b], us.at[k, b], ur.at[k, b],
            device_id=to_z(1), device_id_type=MESH,
        )

    def down_copy(k, b):
        return pltpu.make_async_remote_copy(
            sd.at[k, b], rd.at[k, b], ds.at[k, b], dr.at[k, b],
            device_id=to_z(-1), device_id_type=MESH,
        )

    def go_up(k, b):
        value = part(UP[b] - k, b)
        if k:
            up_copy(k - 1, b).wait_recv()
            value = value + ru[k - 1, b].astype(F32)
        su[k, b] = value.astype(BF16)
        up_copy(k, b).start()

    def go_down(k, b):
        value = part(k - DOWN[b], b)
        if k:
            down_copy(k - 1, b).wait_recv()
            value = value + rd[k - 1, b].astype(F32)
        sd[k, b] = value.astype(BF16)
        down_copy(k, b).start()

    compute(0)
    pl.semaphore_wait(barrier, 3)
    pair_send(0)
    compute(1)
    pair_send(1)
    pair_wait(0)
    go_up(0, 0)
    go_down(0, 1)
    compute(2)
    pair_send(2)
    pair_wait(1)
    go_down(0, 0)
    go_down(1, 1)
    compute(3)
    pair_send(3)
    pair_wait(2)
    go_up(0, 1)
    go_up(1, 0)
    go_down(1, 0)
    go_down(2, 1)
    go_up(1, 1)
    go_up(2, 0)
    pair_wait(3)
    go_down(2, 0)
    go_down(3, 1)
    go_up(2, 1)
    go_up(3, 0)
    for b in range(2):
        total = part(0, b)
        down_copy(DOWN[b] - 1, b).wait_recv()
        total = total + rd[DOWN[b] - 1, b].astype(F32)
        up_copy(UP[b] - 1, b).wait_recv()
        grad[b * PART : (b + 1) * PART, :] = total + ru[UP[b] - 1, b].astype(F32)
    for n in range(4):
        for j in range(2):
            pair_copy(n, j).wait_send()
    for b in range(2):
        for k in range(UP[b]):
            up_copy(k, b).wait_send()
        for k in range(DOWN[b]):
            down_copy(k, b).wait_send()


def reduce_call(rows, hg):
    vmem = pl.BlockSpec(memory_space=pltpu.VMEM)
    hbm = pl.BlockSpec(memory_space=pl.ANY)
    dma = pltpu.SemaphoreType.DMA
    wide = 3 * DH
    return pl.pallas_call(
        reduce_kernel,
        name="grad_reduce",
        out_shape=jax.ShapeDtypeStruct((SHARD, wide), F32),
        in_specs=[hbm, hbm],
        out_specs=vmem,
        scratch_shapes=[
            pltpu.VMEM((GR, wide), BF16),
            dma(()),
            pltpu.VMEM((4, GR, FC), BF16),
            pltpu.VMEM((4, FC, wide), F32),
            pltpu.VMEM((8, SHARD, wide), F32),
            pltpu.VMEM((4, 2, PART, wide), BF16),
            pltpu.VMEM((4, 2, PART, wide), BF16),
            pltpu.VMEM((4, 2, PART, wide), BF16),
            pltpu.VMEM((4, 2, PART, wide), BF16),
            dma((4,)), dma((4, 2)), dma((4, 2)),
            dma((4, 2)), dma((4, 2)), dma((4, 2)), dma((4, 2)),
        ],
        compiler_params=pltpu.CompilerParams(
            collective_id=1, has_side_effects=True, vmem_limit_bytes=VMEM_LIMIT
        ),
    )(rows, hg)


def body(tokens, modulation, img_size, text_count, move_list, w_qkv, qk_gain, cotangent):
    moves = move_list.transpose(1, 2, 0)
    sizes = img_size.T
    gathered, projected, upstream = gather_call(
        sizes, text_count.T, moves, tokens, modulation, w_qkv, cotangent
    )
    attended, head_grads = attention_call(sizes, moves, projected, upstream, qk_gain)
    return (attended, reduce_call(gathered, head_grads))


def solution(mesh):
    placed = (
        P(("dp", "seq"), None),
        P(None, "dp", None),
        P(),
        P(),
        P(),
        P("dp", "seq"),
        P(None, "seq"),
        P(("dp", "seq"), None),
    )
    return jax.shard_map(
        body,
        mesh=mesh,
        in_specs=placed,
        out_specs=(P("dp", "seq"), P("dp", "seq")),
        check_vma=False,
    )
```
